768 devices in a mesh: dp: 16 (over x, y_hi, core), mp: 48 (over y_lo, z).
Axes of the slice: x: 4, y: 8 (y_hi: 2, y_lo: 4; y = y_hi * 4 + y_lo), z: 12, core: 2. Of those that a mesh axis runs over, the one named last changes fastest.
Arguments:
- tokens: bfloat16 [4096, 6144], P('dp', 'mp'), may hold values from -700 to 700
- ln_gain: float32 [6144], replicated, may hold values from 0.1 to 1.9
- w_qkv: bfloat16 [6144, 18432], P(None, 'mp'), may hold values from -1 to 1
- q_gain: float32 [48, 128], P('mp'), may hold values from 0.4 to 7
- k_gain: float32 [48, 128], P('mp'), may hold values from 0.4 to 7
- d_attn: bfloat16 [4096, 6144], P('dp', 'mp'), may hold values from -0.29882812 to 0.29882812
Outputs:
- grad_qkv: bfloat16 [6144, 18432], P('dp', 'mp')
The draws below stay inside these ranges and needn't reach their ends.
All inputs are finite; a program needn't handle non-finite values.
Results may differ from the reference program's by a relative error of at most 0.02.
The reference program's roundings to bfloat16 on the way count: a program that leaves them out, or rounds other values in their place, can miss the bound.
Values may be sent and summed in bfloat16 or wider, within the bound.
A program may use at most 32 MiB of HBM per device.

```python
import math
import jax
import jax.numpy as jnp
from jax import lax

D = 6144
HEADS = 48
HD = 128
SEQ = 256
IMG_DEV = 1
TOKENS = 4096
N_DP = 16


def draw_tokens(key, part):
    key = jax.random.fold_in(key, 11)
    subkeys = jax.random.split(key, 4)
    column_scale = jnp.exp(jax.random.uniform(subkeys[1], (D,), jnp.float32, 0.0, math.log(10.0)))
    row_scale = jnp.exp(jax.random.uniform(subkeys[2], (TOKENS, 1), jnp.float32, 0.0, math.log(10.0)))
    offset = jax.random.truncated_normal(subkeys[3], -6.0, 6.0, (D,), jnp.float32) * 0.5
    base = jax.random.truncated_normal(subkeys[0], -6.0, 6.0, (TOKENS, D), jnp.float32)
    return (row_scale * (base * column_scale + offset)).astype(jnp.bfloat16)


def draw_w_qkv(key, part):
    key = jax.random.fold_in(key, 12)
    subkeys = jax.random.split(key, 1)
    base = jax.random.truncated_normal(subkeys[0], -6.0, 6.0, (D, HEADS, 3, HD), jnp.float32) / math.sqrt(D)
    return base.reshape(D, 3 * HEADS * HD).astype(jnp.bfloat16)


def draw_q_gain(key, part):
    key = jax.random.fold_in(key, 13)
    subkeys = jax.random.split(key, 1)
    return jnp.exp(jax.random.uniform(subkeys[0], (HEADS, HD), jnp.float32, math.log(0.5), math.log(2.0)))


def draw_k_gain(key, part):
    key = jax.random.fold_in(key, 14)
    subkeys = jax.random.split(key, 1)
    return jnp.exp(jax.random.uniform(subkeys[0], (HEADS, HD), jnp.float32, math.log(0.5), math.log(2.0)))


def block_scale(rng, dims, cuts, smallest, high):
    level = 1.0
    for axis_at, blocks in cuts:
        draws = jax.random.uniform(jax.random.fold_in(jax.random.fold_in(rng, 6), axis_at), (blocks,), jnp.float32, smallest / len(cuts), high / len(cuts))
        level = level * jnp.repeat(jnp.exp(draws), dims[axis_at] // blocks).reshape((-1,) + (1,) * (len(dims) - 1 - axis_at))
    return level


def scatter_about(own_key, extent, scale, reach, shards=(), held_as=jnp.bfloat16):
    result = jax.random.normal(own_key, extent, jnp.float32) * scale
    if len(shards) > 0:
        result = block_scale(own_key, extent, shards, -0.22, 0.18) * result
    return jnp.clip(result, min=-reach, max=reach).astype(held_as)


def setup_inputs(seed: int = 0) -> dict:
    streams_of = jax.random.split(jax.random.key(seed), 7)
    return {
        "tokens": draw_tokens(jax.random.fold_in(streams_of[6], 71), 0),
        "ln_gain": jnp.clip(1.0 + 0.18 * jax.random.normal(streams_of[1], (D,), jnp.float32), 0.1, 1.9),
        "w_qkv": draw_w_qkv(jax.random.fold_in(streams_of[6], 71), 0),
        "q_gain": draw_q_gain(jax.random.fold_in(streams_of[6], 71), 0),
        "k_gain": draw_k_gain(jax.random.fold_in(streams_of[6], 71), 0),
        "d_attn": scatter_about(streams_of[5], (TOKENS, HEADS * HD), 0.05, 0.29882812, ((0, 16), (1, 48))),
    }


def norm_rows(activations, gain_row):
    widened = activations.astype(jnp.float32)
    center = lax.optimization_barrier(jnp.mean(widened, axis=-1, keepdims=True))
    spread = lax.optimization_barrier(jnp.mean(jnp.square(widened - center), axis=-1, keepdims=True))
    return (widened - center) * lax.rsqrt(spread + 1e-06) * gain_row

def head_norm(vectors):
    center = lax.optimization_barrier(jnp.mean(vectors, axis=-1, keepdims=True))
    spread = lax.optimization_barrier(jnp.mean(jnp.square(vectors - center), axis=-1, keepdims=True))
    inverse = lax.rsqrt(spread + 1e-06)
    return ((vectors - center) * inverse, inverse)

def head_norm_back(grad_out, normal, inverse, gain_row):
    scaled = grad_out * gain_row
    first = lax.optimization_barrier(jnp.mean(scaled, axis=-1, keepdims=True))
    second = lax.optimization_barrier(jnp.mean(scaled * normal, axis=-1, keepdims=True))
    return inverse * (scaled - first - normal * second)

def reference(tokens, ln_gain, w_qkv, q_gain, k_gain, d_attn):
    row_count = tokens.shape[0]
    images = row_count // SEQ
    normed = norm_rows(tokens, ln_gain).astype(jnp.bfloat16)
    projected = jnp.dot(normed, w_qkv, preferred_element_type=jnp.float32)
    projected = projected.reshape(images, SEQ, HEADS, 3, HD)
    query_hat, query_inv = head_norm(projected[:, :, :, 0])
    key_hat, key_inv = head_norm(projected[:, :, :, 1])
    query_n = (query_hat * q_gain).astype(jnp.bfloat16)
    key_n = (key_hat * k_gain).astype(jnp.bfloat16)
    values = projected[:, :, :, 2].astype(jnp.bfloat16)
    score_scale = 1.0 / math.sqrt(HD)
    scores = jnp.einsum('bihd,bjhd->bhij', query_n.astype(jnp.float32), key_n.astype(jnp.float32)) * score_scale
    probs = jax.nn.softmax(scores, axis=-1)
    probs_low = probs.astype(jnp.bfloat16)
    upstream = d_attn.reshape(images, SEQ, HEADS, HD)
    grad_value = jnp.einsum('bhij,bihd->bjhd', probs_low.astype(jnp.float32), upstream.astype(jnp.float32))
    grad_prob = jnp.einsum('bihd,bjhd->bhij', upstream.astype(jnp.float32), values.astype(jnp.float32))
    grad_score = probs * (grad_prob - lax.optimization_barrier(jnp.sum(probs * grad_prob, axis=-1, keepdims=True)))
    grad_score = (grad_score * score_scale).astype(jnp.bfloat16)
    grad_qn = jnp.einsum('bhij,bjhd->bihd', grad_score.astype(jnp.float32), key_n.astype(jnp.float32))
    grad_kn = jnp.einsum('bhij,bihd->bjhd', grad_score.astype(jnp.float32), query_n.astype(jnp.float32))
    grad_query = head_norm_back(grad_qn, query_hat, query_inv, q_gain)
    grad_key = head_norm_back(grad_kn, key_hat, key_inv, k_gain)
    joined = jnp.stack([grad_query, grad_key, grad_value], axis=3)
    joined = joined.reshape(row_count, 3 * HEADS * HD).astype(jnp.bfloat16)
    group_rows = IMG_DEV * SEQ
    normed_groups = normed.reshape(N_DP, group_rows, D)
    joined_groups = joined.reshape(N_DP, group_rows, 3 * HEADS * HD)

    def accumulate(carry, pieces):
        partial_value = jnp.dot(pieces[0].T, pieces[1], preferred_element_type=jnp.float32).astype(jnp.bfloat16)
        partial_value = lax.optimization_barrier(partial_value)
        return (carry + partial_value.astype(jnp.float32), None)
    summed, _ = lax.scan(accumulate, jnp.zeros((D, 3 * HEADS * HD), jnp.float32), (normed_groups, joined_groups))
    return summed.astype(jnp.bfloat16)
```

```python
import functools
import math

import jax
import jax.numpy as jnp
from jax import lax
from jax.experimental import pallas as pl
from jax.experimental.pallas import tpu as pltpu
from jax.sharding import PartitionSpec as P

MESH = pl.DeviceIdType.MESH
F32 = jnp.float32
BF16 = jnp.bfloat16
SEQ = 256
HD = 128
NX = 4
NYL = 4
NZ = 12
BLOCKS = NYL * NZ
WIDTH = BLOCKS * HD
COLS = 3 * HD
GROUPS = WIDTH // COLS
FAR = NZ // 2
RA = 192
HA = RA // 2
HB = (SEQ - RA) // 2
HALF = COLS // 2


def rdma(src, dst, send, recv, device):
    return pltpu.make_async_remote_copy(
        src_ref=src, dst_ref=dst, send_sem=send, recv_sem=recv, device_id=device, device_id_type=MESH
    )


def head_norm(t):
    center = jnp.mean(t, axis=0, keepdims=True)
    moved = t - center
    spread = jnp.mean(moved * moved, axis=0, keepdims=True)
    inverse = lax.rsqrt(spread + 1e-06)
    return moved * inverse, inverse


def head_norm_back(grad, normal, inverse, gain):
    scaled = grad * gain
    first = jnp.mean(scaled, axis=0, keepdims=True)
    second = jnp.mean(scaled * normal, axis=0, keepdims=True)
    return inverse * (scaled - first - normal * second)


def nt(a, b):
    return lax.dot_general(a, b, (((1,), (1,)), ((), ())), preferred_element_type=F32)


def nn(a, b):
    return jnp.dot(a, b, preferred_element_type=F32)


def body(
    tok, gain, w_hbm, q_gain, k_gain, d_attn, out,
    got, normed, other, w, shift, total, square, proj, joined, joined_other,
    own, part, sx, rx, sy, ry, w_sem,
    s_za, r_za, s_ya, r_ya, s_zb, r_zb, s_yb, r_yb, s_n, r_n, s_j, r_j, s_x, r_x, s_y, r_y,
):
    d = lax.axis_index("dp")
    m = lax.axis_index("mp")
    core = lax.rem(d, 2)
    yh = lax.rem(d // 2, 2)
    x = d // 4
    yl = m // NZ
    z = lax.rem(m, NZ)

    z_dev = [(d, yl * NZ + lax.rem(z + 1, NZ)), (d, yl * NZ + lax.rem(z + NZ - 1, NZ))]
    y_dev = [(d, lax.rem(yl + k, NYL) * NZ + z) for k in (1, 2, 3)]
    x_dev = [
        (lax.rem(x + 1, NX) * 4 + yh * 2 + core, m),
        (lax.rem(x + NX - 1, NX) * 4 + yh * 2 + core, m),
    ]
    core_dev = (d + 1 - 2 * core, m)
    far_dev = (x * 4 + (1 - yh) * 2 + core, m)

    load_w = pltpu.make_async_copy(w_hbm, w, w_sem)
    load_w.start()

    barrier = pltpu.get_barrier_semaphore()
    partners = z_dev + y_dev + x_dev + [core_dev, far_dev]
    for device in partners:
        pl.semaphore_signal(barrier, inc=1, device_id=device, device_id_type=MESH)
    pl.semaphore_wait(barrier, len(partners))

    lines = [yl, yl + 1 - 2 * lax.rem(yl, 2), 2 - yl // 2, 3 - 3 * (yl // 2)]

    def from_z(way, step):
        return lax.rem(z + 2 * NZ - step if way == 0 else z + step, NZ)

    def rows_a(way, last):
        if not last:
            return pl.ds(0, RA)
        return pl.ds(0, HA) if way == 0 else pl.ds(HA, RA - HA)

    def rows_b(way, last):
        if not last:
            return pl.ds(RA, SEQ - RA)
        return pl.ds(RA, HB) if way == 0 else pl.ds(RA + HB, SEQ - RA - HB)

    def za(way, step, k, mine=False, last=False):
        rows = rows_a(way, last)
        block = lines[k] * NZ + from_z(way, step - 1)
        src = tok.at[rows] if mine else got.at[block, rows]
        return rdma(src, got.at[block, rows], s_za.at[way, step - 1, k], r_za.at[way, step - 1, k], z_dev[way])

    def za_in(way, step, k, last=False):
        rows = rows_a(way, last)
        block = lines[k] * NZ + from_z(way, step)
        here = got.at[block, rows]
        return rdma(here, here, s_za.at[way, step - 1, k], r_za.at[way, step - 1, k], z_dev[way])

    def zb(way, step, mine=False, last=False):
        rows = rows_b(way, last)
        block = yl * NZ + from_z(way, step - 1)
        src = tok.at[rows] if mine else got.at[block, rows]
        return rdma(src, got.at[block, rows], s_zb.at[way, step - 1], r_zb.at[way, step - 1], z_dev[way])

    def zb_in(way, step, last=False):
        rows = rows_b(way, last)
        here = got.at[yl * NZ + from_z(way, step), rows]
        return rdma(here, here, s_zb.at[way, step - 1], r_zb.at[way, step - 1], z_dev[way])

    def yb(k, slot, way, step, mine=False, last=False):
        rows = rows_b(way, last)
        block = yl * NZ + from_z(way, step)
        src = tok.at[rows] if mine else got.at[block, rows]
        return rdma(src, got.at[block, rows], s_yb.at[k, slot], r_yb.at[k, slot], y_dev[k])

    def yb_in(k, slot, way, step, last=False):
        rows = rows_b(way, last)
        here = got.at[lax.rem(yl + NYL - 1 - k, NYL) * NZ + from_z(way, step), rows]
        return rdma(here, here, s_yb.at[k, slot], r_yb.at[k, slot], y_dev[k])

    def ya(k):
        rows = pl.ds(0, RA)
        return rdma(tok.at[rows], got.at[m, rows], s_ya.at[k], r_ya.at[k], y_dev[k])

    for way in (0, 1):
        za(way, 1, 0, mine=True).start()
    for k in range(3):
        ya(k).start()
    for way in (0, 1):
        zb(way, 1, mine=True).start()
    for k in range(3):
        yb(k, 0, 0, 0, mine=True).start()

    here = tok[...]
    got[m] = here
    wide = here.astype(F32)
    middle = jnp.mean(wide, axis=1, keepdims=True)
    shift[...] = jnp.broadcast_to(middle, (SEQ, HD))
    moved = wide - middle
    total[...] = moved
    square[...] = moved * moved

    def add_rows(blocks, start, size):
        rows = pl.ds(start, size)
        base = shift[rows]
        first = total[rows]
        second = square[rows]
        for block in blocks:
            v = got[block, rows].astype(F32) - base
            first += v
            second += v * v
        total[rows] = first
        square[rows] = second

    def add_a(blocks):
        for start in range(0, RA, 64):
            add_rows(blocks, start, 64)

    def add_b(blocks):
        add_rows(blocks, RA, SEQ - RA)

    for k in (1, 2, 3):
        line = lines[k]
        at = lax.rem(yl - line + NYL, NYL) - 1
        rows = pl.ds(0, RA)
        ref = got.at[line * NZ + z, rows]
        rdma(ref, ref, s_ya.at[at], r_ya.at[at], z_dev[0]).wait_recv()
        for way in (0, 1):
            za(way, 1, k).start()
    add_a([lines[k] * NZ + z for k in (1, 2, 3)])

    def y_in(slots, far=False):
        blocks = []
        for slot, way, step in slots:
            for k in range(3):
                yb_in(k, slot, way, step, last=far).wait_recv()
                blocks.append(lax.rem(yl + NYL - 1 - k, NYL) * NZ + from_z(way, step))
        return blocks

    def pass_on(step, last):
        for k in range(4):
            for way in (0, 1):
                za_in(way, step, k).wait_recv()
                za(way, step + 1, k, last=last).start()
        for way in (0, 1):
            zb_in(way, step).wait_recv()
            zb(way, step + 1, last=last).start()
        for way in (0, 1):
            for k in range(3):
                yb(k, 2 * step - 1 + way, way, step).start()
        add_a([lines[k] * NZ + from_z(way, step) for k in range(4) for way in (0, 1)])
        add_b([yl * NZ + from_z(way, step) for way in (0, 1)])

    pass_on(1, False)
    add_b(y_in([(0, 0, 0)]))

    def middle_step(step, carry):
        pass_on(step, False)
        add_b(y_in([(2 * step - 3 + way, way, step - 1) for way in (0, 1)]))
        return carry

    lax.fori_loop(2, FAR - 1, middle_step, 0)
    pass_on(FAR - 1, True)
    add_b(y_in([(2 * FAR - 5 + way, way, FAR - 2) for way in (0, 1)]))
    for way in (0, 1):
        zb_in(way, FAR, last=True).wait_recv()
        for k in range(3):
            yb(k, 2 * FAR - 1 + way, way, FAR, last=True).start()
    for k in range(4):
        for way in (0, 1):
            za_in(way, FAR, k, last=True).wait_recv()
    far_z = from_z(0, FAR)
    add_a([lines[k] * NZ + far_z for k in range(4)])
    add_b([yl * NZ + far_z])
    add_b(y_in([(2 * FAR - 3 + way, way, FAR - 1) for way in (0, 1)]))
    blocks = y_in([(2 * FAR - 1, 0, FAR)], far=True)
    y_in([(2 * FAR, 1, FAR)], far=True)
    add_b(blocks)

    mean_moved = jnp.sum(total[...], axis=1, keepdims=True) / WIDTH
    spread = jnp.sum(square[...], axis=1, keepdims=True) / WIDTH - mean_moved * mean_moved
    total[...] = shift[...] + mean_moved
    square[...] = jnp.broadcast_to(lax.rsqrt(spread + 1e-06), (SEQ, HD))
    load_w.wait()

    def norm_copy(p):
        return rdma(normed.at[2 * p + 1 - core], other.at[p], s_n.at[p], r_n.at[p], core_dev)

    for p in range(GROUPS // 2):
        center = total[...]
        scale = square[...]
        pieces = []
        for group in (2 * p + 1 - core, 2 * p + core):
            for b in range(3):
                block = 3 * group + b
                v = (got[block].astype(F32) - center) * scale * gain[block]
                v = v.astype(BF16)
                normed[group, :, b * HD : (b + 1) * HD] = v
                pieces.append(v)
        norm_copy(p).start()
        left = jnp.concatenate(pieces, axis=1)
        right = jnp.concatenate([w[2 * p + 1 - core], w[2 * p + core]], axis=0)
        term = nn(left, right)
        if p == 0:
            proj[...] = term
        else:
            proj[...] += term

    score_scale = 1.0 / math.sqrt(HD)
    gain_q = jnp.broadcast_to(q_gain[...], (HD, HD)).T
    gain_k = jnp.broadcast_to(k_gain[...], (HD, HD)).T
    gain_q = jnp.concatenate([gain_q, gain_q], axis=1)
    gain_k = jnp.concatenate([gain_k, gain_k], axis=1)
    up_t = d_attn[...].astype(F32).T.astype(BF16)
    q_t = proj[:, 0:HD].T
    k_t = proj[:, HD : 2 * HD].T
    values = proj[:, 2 * HD :].astype(BF16)
    q_hat, q_inv = head_norm(q_t)
    k_hat, k_inv = head_norm(k_t)
    q_n_t = (q_hat * gain_q).astype(BF16)
    k_n_f = k_hat * gain_k
    k_n_t = k_n_f.astype(BF16)
    k_n = k_n_f.T.astype(BF16)
    scores = nn(k_n, q_n_t) * score_scale
    grad_prob = nn(values, up_t)
    raised = jnp.exp(scores - jnp.max(scores, axis=0, keepdims=True))
    probs = raised / jnp.sum(raised, axis=0, keepdims=True)
    probs_low = probs.astype(BF16)
    grad_score = probs * (grad_prob - jnp.sum(probs * grad_prob, axis=0, keepdims=True))
    grad_score = (grad_score * score_scale).astype(BF16)
    grad_v = nt(up_t, probs_low)
    grad_kn = nt(q_n_t, grad_score)
    grad_qn = nn(k_n_t, grad_score)
    joined[0:HD] = head_norm_back(grad_qn, q_hat, q_inv, gain_q).astype(BF16)
    joined[HD : 2 * HD] = head_norm_back(grad_kn, k_hat, k_inv, gain_k).astype(BF16)
    joined[2 * HD :] = grad_v.astype(BF16)
    send_j = rdma(joined, joined_other, s_j.at[0], r_j.at[0], core_dev)
    send_j.start()
    for p in range(GROUPS // 2):
        norm_copy(p).wait_recv()
    send_j.wait_recv()

    def grad_part(x_to, y_to, half):
        rows = pl.ds(half * HALF, HALF)
        left = jnp.concatenate([joined[rows], joined_other[rows]], axis=1)
        at = x_to * 2 + y_to
        right = jnp.concatenate([normed[at * 2 + core], other[at]], axis=0)
        return nn(left, right)

    def x_copy(i, way, kind):
        return rdma(sx.at[i, way, kind], rx.at[i, way, kind], s_x.at[i, way, kind], r_x.at[i, way, kind], x_dev[way])

    x_next = [lax.rem(x + 1, NX), lax.rem(x + NX - 1, NX)]
    x_far = lax.rem(x + 2, NX)

    def first_parts(i, y_to, send):
        for way in (0, 1):
            sx[i, way, 0] = grad_part(x_far, y_to, way).astype(BF16)
            if send:
                x_copy(i, way, 0).start()
        for way in (0, 1):
            sx[i, way, 1] = grad_part(x_next[way], y_to, 1 - way).astype(BF16)
            if send:
                x_copy(i, way, 1).start()

    def later_parts(i, y_to):
        for way in (0, 1):
            part[i, way] = grad_part(x_next[way], y_to, way)
        for half in (0, 1):
            own[i, half] = grad_part(x, y_to, half)

    def relay(i):
        for way in (0, 1):
            x_copy(i, way, 0).wait_recv()
            sx[i, way, 2] = (part[i, way] + rx[i, way, 0].astype(F32)).astype(BF16)
            x_copy(i, way, 2).start()

    def gather_half(i, half):
        x_copy(i, 1 - half, 1).wait_recv()
        x_copy(i, half, 2).wait_recv()
        return own[i, half] + rx[i, 1 - half, 1].astype(F32) + rx[i, half, 2].astype(F32)

    def y_copy(half):
        return rdma(sy.at[half], ry.at[half], s_y.at[half], r_y.at[half], far_dev)

    first_parts(0, 1 - yh, True)
    later_parts(0, 1 - yh)
    first_parts(1, yh, False)
    later_parts(1, yh)
    relay(0)
    for kind in (0, 1):
        for way in (0, 1):
            x_copy(1, way, kind).start()
    for half in (0, 1):
        sy[half] = gather_half(0, half).astype(BF16)
        y_copy(half).start()
    relay(1)

    for way in (0, 1):
        for k in range(4):
            for step in range(1, FAR + 1):
                za(way, step, k, last=step == FAR).wait_send()
        for step in range(1, FAR + 1):
            zb(way, step, last=step == FAR).wait_send()
    for k in range(3):
        ya(k).wait_send()
        yb(k, 0, 0, 0, mine=True).wait_send()
        for step in range(1, FAR + 1):
            for way in (0, 1):
                yb(k, 2 * step - 1 + way, way, step, last=step == FAR).wait_send()
    for p in range(GROUPS // 2):
        norm_copy(p).wait_send()
    send_j.wait_send()

    for half in (0, 1):
        own[1, half] = gather_half(1, half)
    for half in (0, 1):
        y_copy(half).wait_recv()
        final = own[1, half] + ry[half].astype(F32)
        out[:, half * HALF : (half + 1) * HALF] = final.T.astype(BF16)
    for i in (0, 1):
        for way in (0, 1):
            for kind in (0, 1, 2):
                x_copy(i, way, kind).wait_send()
    for half in (0, 1):
        y_copy(half).wait_send()


def local(tokens, ln_gain, w_qkv, q_gain, k_gain, d_attn):
    dma = pltpu.SemaphoreType.DMA
    vmem = pl.BlockSpec(memory_space=pltpu.VMEM)
    steps = 2 * FAR + 1
    pairs = []
    for shape in ((2, FAR, 4), (3,), (2, FAR), (3, steps), (GROUPS // 2,), (1,), (2, 2, 3), (2,)):
        pairs += [dma(shape), dma(shape)]
    return pl.pallas_call(
        body,
        out_shape=jax.ShapeDtypeStruct((COLS, COLS), BF16),
        in_specs=[vmem, vmem, pl.BlockSpec(memory_space=pl.ANY), vmem, vmem, vmem],
        out_specs=vmem,
        scratch_shapes=[
            pltpu.VMEM((BLOCKS, SEQ, HD), BF16),
            pltpu.VMEM((GROUPS, SEQ, COLS), BF16),
            pltpu.VMEM((GROUPS // 2, SEQ, COLS), BF16),
            pltpu.VMEM((GROUPS, COLS, COLS), BF16),
            pltpu.VMEM((SEQ, HD), F32),
            pltpu.VMEM((SEQ, HD), F32),
            pltpu.VMEM((SEQ, HD), F32),
            pltpu.VMEM((SEQ, COLS), F32),
            pltpu.VMEM((COLS, SEQ), BF16),
            pltpu.VMEM((COLS, SEQ), BF16),
            pltpu.VMEM((2, 2, HALF, COLS), F32),
            pltpu.VMEM((2, 2, HALF, COLS), F32),
            pltpu.VMEM((2, 2, 3, HALF, COLS), BF16),
            pltpu.VMEM((2, 2, 3, HALF, COLS), BF16),
            pltpu.VMEM((2, HALF, COLS), BF16),
            pltpu.VMEM((2, HALF, COLS), BF16),
            dma(()),
        ] + pairs,
        compiler_params=pltpu.CompilerParams(
            collective_id=0, has_side_effects=True, vmem_limit_bytes=48 * 2**20
        ),
        cost_estimate=pl.CostEstimate(flops=2_600_000_000, bytes_accessed=10_000_000, transcendentals=100_000),
        name="layer",
    )(
        tokens, ln_gain.reshape(BLOCKS, 1, HD), w_qkv.reshape(GROUPS, COLS, COLS), q_gain, k_gain, d_attn
    )


def solution(mesh):
    placed = (P("dp", "mp"), P(), P(None, "mp"), P("mp", None), P("mp", None), P("dp", "mp"))
    return jax.shard_map(
        local, mesh=mesh, in_specs=placed, out_specs=P("dp", "mp"), check_vma=False
    )
```

```python
import math

import jax
import jax.numpy as jnp
from jax import lax
from jax.experimental import pallas as pl
from jax.experimental.pallas import tpu as pltpu
from jax.sharding import PartitionSpec as P

MESH = pl.DeviceIdType.MESH
F32 = jnp.float32
BF16 = jnp.bfloat16
SEQ = 256
HD = 128
NX = 4
NYL = 4
NZ = 12
BLOCKS = NYL * NZ
WIDTH = BLOCKS * HD
COLS = 3 * HD
SLOTS = NZ // 2
FAR = NZ // 2
RA = 160
HA = RA // 2
HB = (SEQ - RA) // 2
HALF = COLS // 2
QUARTER = COLS // 4


def rdma(src, dst, send, recv, device):
    return pltpu.make_async_remote_copy(
        src_ref=src, dst_ref=dst, send_sem=send, recv_sem=recv, device_id=device, device_id_type=MESH
    )


def head_norm(t):
    center = jnp.mean(t, axis=0, keepdims=True)
    moved = t - center
    spread = jnp.mean(moved * moved, axis=0, keepdims=True)
    inverse = lax.rsqrt(spread + 1e-06)
    return moved * inverse, inverse


def head_norm_back(grad, normal, inverse, gain):
    scaled = grad * gain
    first = jnp.mean(scaled, axis=0, keepdims=True)
    second = jnp.mean(scaled * normal, axis=0, keepdims=True)
    return inverse * (scaled - first - normal * second)


def nt(a, b):
    return lax.dot_general(a, b, (((1,), (1,)), ((), ())), preferred_element_type=F32)


def nn(a, b):
    return jnp.dot(a, b, preferred_element_type=F32)


def merge(parts, count):
    mean = sum(p[0:2] for p in parts) / len(parts)
    spread = sum(p[2:4] for p in parts)
    moved = [p[0:2] - mean for p in parts]
    return mean, spread + count * sum(v * v for v in moved)


def body(
    tok, gain_in, w_in, q_gain_in, k_gain_in, d_attn_in, out,
    got, normed, other, w, gain, q_gain, k_gain, d_attn,
    stat, stat_y, stat_4, stat_z, center, scale, proj, joined, joined_other, up_t, gains_t,
    own, part, sx, rx, sy, ry, loads,
    s_za, r_za, s_ya, r_ya, s_zb, r_zb, s_yb, r_yb, s_sy, r_sy, s_sz, r_sz, s_n, r_n, s_j, r_j, s_x, r_x, s_y, r_y,
    s_yr,
):
    d = lax.axis_index("dp")
    m = lax.axis_index("mp")
    core = lax.rem(d, 2)
    yh = lax.rem(d // 2, 2)
    x = d // 4
    yl = m // NZ
    z = lax.rem(m, NZ)

    def z_at(hops):
        return (d, yl * NZ + lax.rem(z + hops, NZ))

    z_dev = [z_at(1), z_at(NZ - 1)]
    y_dev = [(d, lax.rem(yl + k, NYL) * NZ + z) for k in (1, 2, 3)]
    x_dev = [
        (lax.rem(x + 1, NX) * 4 + yh * 2 + core, m),
        (lax.rem(x + NX - 1, NX) * 4 + yh * 2 + core, m),
    ]
    core_dev = (d + 1 - 2 * core, m)
    far_dev = (x * 4 + (1 - yh) * 2 + core, m)

    def load(i, src, dst):
        return pltpu.make_async_copy(src, dst, loads.at[i])

    load_tok = load(0, tok, got.at[z, yl])
    load_w = load(1, w_in, w)
    small = [load(2, gain_in, gain), load(3, q_gain_in, q_gain), load(4, k_gain_in, k_gain), load(5, d_attn_in, d_attn)]
    load_tok.start()

    barrier = pltpu.get_barrier_semaphore()
    partners = [z_at(hops) for hops in range(1, NZ)] + y_dev + x_dev + [core_dev, far_dev]
    for device in partners:
        pl.semaphore_signal(barrier, inc=1, device_id=device, device_id_type=MESH)

    load_tok.wait()
    for copy in small:
        copy.start()
    load_w.start()
    turned = got[z, yl].astype(F32).T
    mean = jnp.mean(turned, axis=0, keepdims=True)
    moved = turned - mean
    spread = jnp.sum(moved * moved, axis=0, keepdims=True)
    stat[0:1] = mean[:, :HD]
    stat[1:2] = mean[:, HD:]
    stat[2:3] = spread[:, :HD]
    stat[3:4] = spread[:, HD:]
    pl.semaphore_wait(barrier, len(partners))

    lines = [yl, yl + 1 - 2 * lax.rem(yl, 2), 2 - yl // 2, 3 - 3 * (yl // 2)]

    def from_z(way, step):
        return lax.rem(z + 2 * NZ - step if way == 0 else z + step, NZ)

    def rows_a(way, step):
        if step < FAR:
            return pl.ds(0, RA)
        return pl.ds(0, HA) if way == 0 else pl.ds(HA, RA - HA)

    def rows_b(way, step):
        if step < FAR:
            return pl.ds(RA, SEQ - RA)
        return pl.ds(RA, HB) if way == 0 else pl.ds(RA + HB, SEQ - RA - HB)

    def za(way, step, k):
        rows = rows_a(way, step)
        at = from_z(way, step - 1)
        src = tok.at[rows] if step == 1 and k == 0 else got.at[at, lines[k], rows]
        return rdma(src, got.at[at, lines[k], rows], s_za.at[way, step - 1, k], r_za.at[way, step - 1, k], z_dev[way])

    def za_in(way, step, k):
        here = got.at[from_z(way, step), lines[k], rows_a(way, step)]
        return rdma(here, here, s_za.at[way, step - 1, k], r_za.at[way, step - 1, k], z_dev[way])

    def zb(way, step):
        rows = rows_b(way, step)
        at = from_z(way, step - 1)
        src = tok.at[rows] if step == 1 else got.at[at, yl, rows]
        return rdma(src, got.at[at, yl, rows], s_zb.at[way, step - 1], r_zb.at[way, step - 1], z_dev[way])

    def zb_in(way, step):
        here = got.at[from_z(way, step), yl, rows_b(way, step)]
        return rdma(here, here, s_zb.at[way, step - 1], r_zb.at[way, step - 1], z_dev[way])

    def slot_of(way, step):
        return 2 * step - 1 + way if step else 0

    def yb(k, way, step):
        rows = rows_b(way, step)
        at = from_z(way, step)
        slot = slot_of(way, step)
        src = tok.at[rows] if step == 0 else got.at[at, yl, rows]
        return rdma(src, got.at[at, yl, rows], s_yb.at[k, slot], r_yb.at[k, slot], y_dev[k])

    def yb_in(k, way, step):
        slot = slot_of(way, step)
        here = got.at[from_z(way, step), lax.rem(yl + NYL - 1 - k, NYL), rows_b(way, step)]
        return rdma(here, here, s_yb.at[k, slot], r_yb.at[k, slot], y_dev[k])

    def yb_relay(way, step):
        slot = slot_of(way, step)
        here = got.at[from_z(way, step), lax.rem(yl + 2, NYL), rows_b(way, step)]
        return rdma(here, here, s_yr.at[slot], r_yb.at[2 * (yl - 1), slot], (d, 3 * (yl - 1) * NZ + z))

    inner = jnp.logical_and(yl > 0, yl < NYL - 1)

    def each_yb(way, step, act):
        act(yb(1, way, step))

        @pl.when(yl < NYL - 1)
        def _():
            act(yb(0, way, step))

        @pl.when(yl > 0)
        def _():
            act(yb(2, way, step))

    def start(copy):
        copy.start()

    def wait_send(copy):
        copy.wait_send()

    def ya(k):
        rows = pl.ds(0, RA)
        at = lax.rem(lines[k] - yl + NYL, NYL) - 1
        return rdma(tok.at[rows], got.at[z, yl, rows], s_ya.at[at], r_ya.at[at], (d, lines[k] * NZ + z))

    def ya_in(k):
        at = lax.rem(yl - lines[k] + NYL, NYL) - 1
        here = got.at[z, lines[k], pl.ds(0, RA)]
        return rdma(here, here, s_ya.at[at], r_ya.at[at], z_dev[0])

    def stat_y_copy(k):
        return rdma(stat, stat_y.at[k], s_sy.at[k], r_sy.at[k], y_dev[k])

    def stat_z_copy(hops):
        return rdma(stat_4, stat_z.at[hops - 1], s_sz.at[hops - 1], r_sz.at[hops - 1], z_at(hops))

    for k in range(3):
        stat_y_copy(k).start()
    for way in (0, 1):
        za(way, 1, 0).start()
    for k in (1, 2, 3):
        ya(k).start()
    for way in (0, 1):
        zb(way, 1).start()
    each_yb(0, 0, start)

    for k in range(3):
        stat_y_copy(k).wait_recv()
    mean, spread = merge([stat[...]] + [stat_y[k] for k in range(3)], HD)
    stat_4[0:2] = mean
    stat_4[2:4] = spread
    for hops in range(1, NZ):
        stat_z_copy(hops).start()

    def z_pass(step, k):
        for way in (0, 1):
            za_in(way, step, k).wait_recv()
            if step < FAR:
                za(way, step + 1, k).start()

    def b_pass(step):
        for way in (0, 1):
            zb_in(way, step).wait_recv()
            if step < FAR:
                zb(way, step + 1).start()
            each_yb(way, step, start)

    def y_in(step):
        for way in (0, 1) if step else (0,):
            yb_in(1, way, step).wait_recv()

            @pl.when(inner)
            def _():
                yb_relay(way, step).start()

        for way in (0, 1) if step else (0,):
            for k in (0, 2):
                yb_in(k, way, step).wait_recv()

    def swap(zz):
        slot = zz // 6 * 3 + lax.rem(zz, 3)
        return rdma(normed.at[zz], other.at[slot], s_n.at[slot], r_n.at[slot], core_dev)

    def process(step):
        places = [from_z(way, step) for way in (0, 1)]
        if step == 0 or step == FAR:
            places = places[:1]
        middle = center[...]
        factor = scale[...]
        left, right = [], []
        for zz in places:
            for line in range(NYL):
                block = line * NZ + zz
                v = (got[zz, line].astype(F32) - middle) * factor * gain[block]
                v = v.astype(BF16)
                normed[zz, line] = v
                left.append(v)
                right.append(w[block])
        term = nn(jnp.concatenate(left, axis=1), jnp.concatenate(right, axis=0))
        if step == 0:
            proj[...] = term
        else:
            proj[...] += term
        for zz in places:

            @pl.when(lax.rem(zz // 3, 2) != core)
            def _():
                swap(zz).start()

    b_pass(1)
    z_pass(1, 0)
    for k in (1, 2, 3):
        ya_in(k).wait_recv()
        for way in (0, 1):
            za(way, 1, k).start()
    b_pass(2)
    y_in(0)
    for copy in small:
        copy.wait()
    for i, ref in enumerate((q_gain, k_gain)):
        column = jnp.broadcast_to(ref[...], (HD, HD)).T
        gains_t[i] = jnp.concatenate([column, column], axis=1)
    up_t[...] = d_attn[...].astype(F32).T.astype(BF16)

    b_pass(3)
    z_pass(2, 0)
    for k in (1, 2, 3):
        z_pass(1, k)
    b_pass(4)
    y_in(1)
    for hops in range(1, NZ):
        stat_z_copy(hops).wait_recv()
    mean, spread = merge([stat_4[...]] + [stat_z[hops - 1] for hops in range(1, NZ)], NYL * HD)
    factor = lax.rsqrt(spread / WIDTH + 1e-06)
    for i in (0, 1):
        rows = pl.ds(i * HD, HD)
        center[rows] = jnp.broadcast_to(mean[i : i + 1], (HD, HD)).T
        scale[rows] = jnp.broadcast_to(factor[i : i + 1], (HD, HD)).T
    load_w.wait()
    process(0)

    b_pass(5)
    z_pass(3, 0)
    for k in (1, 2, 3):
        z_pass(2, k)
    b_pass(6)
    y_in(2)
    process(1)
    y_in(3)

    z_pass(4, 0)
    for k in (1, 2, 3):
        z_pass(3, k)
    y_in(4)
    process(2)
    z_pass(5, 0)
    for k in (1, 2, 3):
        z_pass(4, k)
    y_in(5)
    process(3)
    z_pass(6, 0)
    for k in (1, 2, 3):
        z_pass(5, k)
    process(4)
    y_in(6)
    process(5)
    for k in (1, 2, 3):
        z_pass(6, k)
    process(6)

    score_scale = 1.0 / math.sqrt(HD)
    gain_q = gains_t[0]
    gain_k = gains_t[1]
    q_t = proj[:, 0:HD].T
    k_t = proj[:, HD : 2 * HD].T
    values = proj[:, 2 * HD :].astype(BF16)
    q_hat, q_inv = head_norm(q_t)
    k_hat, k_inv = head_norm(k_t)
    q_n_t = (q_hat * gain_q).astype(BF16)
    k_n_f = k_hat * gain_k
    k_n_t = k_n_f.astype(BF16)
    k_n = k_n_f.T.astype(BF16)
    scores = nn(k_n, q_n_t) * score_scale
    grad_prob = nn(values, up_t[...])
    raised = jnp.exp(scores - jnp.max(scores, axis=0, keepdims=True))
    probs = raised / jnp.sum(raised, axis=0, keepdims=True)
    probs_low = probs.astype(BF16)
    grad_score = probs * (grad_prob - jnp.sum(probs * grad_prob, axis=0, keepdims=True))
    grad_score = (grad_score * score_scale).astype(BF16)
    grad_v = nt(up_t[...], probs_low)
    grad_kn = nt(q_n_t, grad_score)
    grad_qn = nn(k_n_t, grad_score)
    joined[0:HD] = head_norm_back(grad_qn, q_hat, q_inv, gain_q).astype(BF16)
    joined[HD : 2 * HD] = head_norm_back(grad_kn, k_hat, k_inv, gain_k).astype(BF16)
    joined[2 * HD :] = grad_v.astype(BF16)
    send_j = rdma(joined, joined_other, s_j.at[0], r_j.at[0], core_dev)
    send_j.start()

    def swap_in(slot):
        return rdma(other.at[slot], other.at[slot], s_n.at[slot], r_n.at[slot], core_dev)

    for slot in range(SLOTS):
        swap_in(slot).wait_recv()
    send_j.wait_recv()

    def grad_part(x_to, y_to, half):
        rows = pl.ds(half * HALF, HALF)
        left = jnp.concatenate([joined[rows], joined_other[rows]], axis=1)
        mine = jnp.concatenate([normed[3 * (2 * y_to + core) + b, x_to] for b in range(3)], axis=1)
        theirs = jnp.concatenate([other[3 * y_to + b, x_to] for b in range(3)], axis=1)
        return nn(left, jnp.concatenate([mine, theirs], axis=0))

    x_next = [lax.rem(x + 1, NX), lax.rem(x + NX - 1, NX)]
    x_far = lax.rem(x + 2, NX)

    def x_copy(i, way, kind, q):
        at = (i, way, kind, q)
        return rdma(sx.at[at], rx.at[at], s_x.at[at], r_x.at[at], x_dev[way])

    def put(i, way, kind, value):
        value = value.astype(BF16)
        for q in (0, 1):
            sx[i, way, kind, q] = value[q * QUARTER : (q + 1) * QUARTER]

    def x_start(i, kind, q):
        for way in (0, 1):
            x_copy(i, way, kind, q).start()

    def relay(i, q):
        for way in (0, 1):
            x_copy(i, way, 0, q).wait_recv()
            sx[i, way, 2, q] = (part[i, way, q] + rx[i, way, 0, q].astype(F32)).astype(BF16)
            x_copy(i, way, 2, q).start()

    def later_parts(i, y_to):
        for way in (0, 1):
            value = grad_part(x_next[way], y_to, way)
            for q in (0, 1):
                part[i, way, q] = value[q * QUARTER : (q + 1) * QUARTER]
        for half in (0, 1):
            value = grad_part(x, y_to, half)
            for q in (0, 1):
                own[i, half, q] = value[q * QUARTER : (q + 1) * QUARTER]

    def gathered(i, half, q):
        x_copy(i, 1 - half, 1, q).wait_recv()
        x_copy(i, half, 2, q).wait_recv()
        return own[i, half, q] + rx[i, 1 - half, 1, q].astype(F32) + rx[i, half, 2, q].astype(F32)

    def y_copy(half, q):
        at = (half, q)
        return rdma(sy.at[at], ry.at[at], s_y.at[at], r_y.at[at], far_dev)

    def y_start(q):
        for half in (0, 1):
            sy[half, q] = gathered(0, half, q).astype(BF16)
            y_copy(half, q).start()

    for way in (0, 1):
        put(0, way, 0, grad_part(x_far, 1 - yh, way))
        x_copy(0, way, 0, 0).start()
    for way in (0, 1):
        put(0, way, 1, grad_part(x_next[way], 1 - yh, 1 - way))
        x_copy(0, way, 1, 0).start()
    x_start(0, 0, 1)
    later_parts(0, 1 - yh)
    for way in (0, 1):
        put(1, way, 0, grad_part(x_far, yh, way))
        put(1, way, 1, grad_part(x_next[way], yh, 1 - way))
    relay(0, 0)
    x_start(0, 1, 1)
    later_parts(1, yh)
    relay(0, 1)
    x_start(1, 0, 0)
    x_start(1, 1, 0)
    x_start(1, 0, 1)
    y_start(0)
    relay(1, 0)
    x_start(1, 1, 1)
    y_start(1)
    relay(1, 1)

    for way in (0, 1):
        for k in range(4):
            for step in range(1, FAR + 1):
                za(way, step, k).wait_send()
        for step in range(1, FAR + 1):
            zb(way, step).wait_send()
    for k in (1, 2, 3):
        ya(k).wait_send()
    for k in range(3):
        stat_y_copy(k).wait_send()
    for hops in range(1, NZ):
        stat_z_copy(hops).wait_send()
    arrivals = [(0, 0)] + [(way, step) for step in range(1, FAR + 1) for way in (0, 1)]
    for way, step in arrivals:
        yb(1, way, step).wait_send()

    @pl.when(yl < NYL - 1)
    def _():
        for way, step in arrivals:
            yb(0, way, step).wait_send()

    @pl.when(yl > 0)
    def _():
        for way, step in arrivals:
            yb(2, way, step).wait_send()

    @pl.when(inner)
    def _():
        for way, step in arrivals:
            yb_relay(way, step).wait_send()

    for slot in range(SLOTS):
        swap_in(slot).wait_send()
    send_j.wait_send()

    final = []
    for half in (0, 1):
        for q in (0, 1):
            value = gathered(1, half, q)
            y_copy(half, q).wait_recv()
            final.append(value + ry[half, q].astype(F32))
    final = jnp.concatenate(final, axis=0)
    for b in range(3):
        out[:, b * HD : (b + 1) * HD] = final[b * HD : (b + 1) * HD].T.astype(BF16)
    for i in (0, 1):
        for way in (0, 1):
            for kind in (0, 1, 2):
                for q in (0, 1):
                    x_copy(i, way, kind, q).wait_send()
    for half in (0, 1):
        for q in (0, 1):
            y_copy(half, q).wait_send()


def local(tokens, ln_gain, w_qkv, q_gain, k_gain, d_attn):
    dma = pltpu.SemaphoreType.DMA
    hbm = pl.BlockSpec(memory_space=pltpu.HBM)
    steps = 2 * FAR + 1
    pairs = []
    for shape in (
        (2, FAR, 4), (3,), (2, FAR), (3, steps), (3,), (NZ - 1,), (SLOTS,), (1,), (2, 2, 3, 2), (2, 2),
    ):
        pairs += [dma(shape), dma(shape)]
    return pl.pallas_call(
        body,
        out_shape=jax.ShapeDtypeStruct((COLS, COLS), BF16),
        in_specs=[hbm] * 6,
        out_specs=pl.BlockSpec(memory_space=pltpu.VMEM),
        scratch_shapes=[
            pltpu.VMEM((NZ, NYL, SEQ, HD), BF16),
            pltpu.VMEM((NZ, NYL, SEQ, HD), BF16),
            pltpu.VMEM((SLOTS, NYL, SEQ, HD), BF16),
            pltpu.VMEM((BLOCKS, HD, COLS), BF16),
            pltpu.VMEM((BLOCKS, 1, HD), F32),
            pltpu.VMEM((1, HD), F32),
            pltpu.VMEM((1, HD), F32),
            pltpu.VMEM((SEQ, HD), BF16),
            pltpu.VMEM((4, HD), F32),
            pltpu.VMEM((3, 4, HD), F32),
            pltpu.VMEM((4, HD), F32),
            pltpu.VMEM((NZ - 1, 4, HD), F32),
            pltpu.VMEM((SEQ, HD), F32),
            pltpu.VMEM((SEQ, HD), F32),
            pltpu.VMEM((SEQ, COLS), F32),
            pltpu.VMEM((COLS, SEQ), BF16),
            pltpu.VMEM((COLS, SEQ), BF16),
            pltpu.VMEM((HD, SEQ), BF16),
            pltpu.VMEM((2, HD, SEQ), F32),
            pltpu.VMEM((2, 2, 2, QUARTER, COLS), F32),
            pltpu.VMEM((2, 2, 2, QUARTER, COLS), F32),
            pltpu.VMEM((2, 2, 3, 2, QUARTER, COLS), BF16),
            pltpu.VMEM((2, 2, 3, 2, QUARTER, COLS), BF16),
            pltpu.VMEM((2, 2, QUARTER, COLS), BF16),
            pltpu.VMEM((2, 2, QUARTER, COLS), BF16),
            dma((6,)),
        ] + pairs + [dma((steps,))],
        compiler_params=pltpu.CompilerParams(
            collective_id=0, has_side_effects=True, vmem_limit_bytes=60 * 2**20
        ),
        cost_estimate=pl.CostEstimate(flops=2_600_000_000, bytes_accessed=10_000_000, transcendentals=100_000),
        name="layer",
    )(
        tokens, ln_gain.reshape(BLOCKS, 1, HD), w_qkv.reshape(BLOCKS, HD, COLS), q_gain, k_gain, d_attn
    )


def solution(mesh):
    placed = (P("dp", "mp"), P(), P(None, "mp"), P("mp", None), P("mp", None), P("dp", "mp"))
    return jax.shard_map(
        local, mesh=mesh, in_specs=placed, out_specs=P("dp", "mp"), check_vma=False
    )
```

```python
import math

import jax
import jax.numpy as jnp
from jax import lax
from jax.experimental import pallas as pl
from jax.experimental.pallas import tpu as pltpu
from jax.sharding import PartitionSpec as P

MESH = pl.DeviceIdType.MESH
F32 = jnp.float32
BF16 = jnp.bfloat16
SEQ = 256
HD = 128
NX = 4
NYL = 4
NZ = 12
BLOCKS = NYL * NZ
WIDTH = BLOCKS * HD
COLS = 3 * HD
SLOTS = NZ // 2
FAR = NZ // 2
RA = 176
HA = 96
HB = 48
HALF = COLS // 2
QUARTER = COLS // 4


def rdma(src, dst, send, recv, device):
    return pltpu.make_async_remote_copy(
        src_ref=src, dst_ref=dst, send_sem=send, recv_sem=recv, device_id=device, device_id_type=MESH
    )


def head_norm(t):
    center = jnp.mean(t, axis=0, keepdims=True)
    moved = t - center
    spread = jnp.mean(moved * moved, axis=0, keepdims=True)
    inverse = lax.rsqrt(spread + 1e-06)
    return moved * inverse, inverse


def head_norm_back(grad, normal, inverse, gain):
    scaled = grad * gain
    first = jnp.mean(scaled, axis=0, keepdims=True)
    second = jnp.mean(scaled * normal, axis=0, keepdims=True)
    return inverse * (scaled - first - normal * second)


def nt(a, b):
    return lax.dot_general(a, b, (((1,), (1,)), ((), ())), preferred_element_type=F32)


def nn(a, b):
    return jnp.dot(a, b, preferred_element_type=F32)


def body(
    tok, gain_in, w_in, q_gain_in, k_gain_in, d_attn_in, out,
    got, other, w, gain, q_gain, k_gain, d_attn,
    shift, total, square, joined, joined_other, mean_own, mean_other, drift, up_t, gains_t,
    own, part, sx, rx, sy, ry, loads,
    s_za, r_za, s_ya, r_ya, s_zb, r_zb, s_yb, r_yb, s_n, r_n, s_m, r_m, s_j, r_j, s_x, r_x, s_y, r_y,
):
    d = lax.axis_index("dp")
    m = lax.axis_index("mp")
    core = lax.rem(d, 2)
    yh = lax.rem(d // 2, 2)
    x = d // 4
    yl = m // NZ
    z = lax.rem(m, NZ)

    z_dev = [(d, yl * NZ + lax.rem(z + hops, NZ)) for hops in (1, NZ - 1)]
    y_dev = [(d, lax.rem(yl + k, NYL) * NZ + z) for k in (1, 2, 3)]
    x_dev = [
        (lax.rem(x + 1, NX) * 4 + yh * 2 + core, m),
        (lax.rem(x + NX - 1, NX) * 4 + yh * 2 + core, m),
    ]
    core_dev = (d + 1 - 2 * core, m)
    far_dev = (x * 4 + (1 - yh) * 2 + core, m)

    def load(i, src, dst):
        return pltpu.make_async_copy(src, dst, loads.at[i])

    load_tok = load(0, tok, got.at[z, yl])
    load_w = load(1, w_in, w)
    small = [load(2, gain_in, gain), load(3, q_gain_in, q_gain), load(4, k_gain_in, k_gain), load(5, d_attn_in, d_attn)]
    load_tok.start()
    for copy in small:
        copy.start()
    load_w.start()

    barrier = pltpu.get_barrier_semaphore()
    partners = z_dev + y_dev + x_dev + [core_dev, far_dev]
    for device in partners:
        pl.semaphore_signal(barrier, inc=1, device_id=device, device_id_type=MESH)

    pl.semaphore_wait(barrier, len(partners))

    lines = [yl, yl + 1 - 2 * lax.rem(yl, 2), 2 - yl // 2, 3 - 3 * (yl // 2)]

    def from_z(way, step):
        return lax.rem(z + 2 * NZ - step if way == 0 else z + step, NZ)

    def rows_a(way, step):
        if step < FAR:
            return pl.ds(0, RA)
        return pl.ds(0, HA) if way == 0 else pl.ds(HA, RA - HA)

    def rows_b(way, step):
        if step < FAR:
            return pl.ds(RA, SEQ - RA)
        return pl.ds(RA, HB) if way == 0 else pl.ds(RA + HB, SEQ - RA - HB)

    def za(way, step, k):
        rows = rows_a(way, step)
        at = from_z(way, step - 1)
        src = tok.at[rows] if step == 1 and k == 0 else got.at[at, lines[k], rows]
        return rdma(src, got.at[at, lines[k], rows], s_za.at[way, step - 1, k], r_za.at[way, step - 1, k], z_dev[way])

    def za_in(way, step, k):
        here = got.at[from_z(way, step), lines[k], rows_a(way, step)]
        return rdma(here, here, s_za.at[way, step - 1, k], r_za.at[way, step - 1, k], z_dev[way])

    def zb(way, step):
        rows = rows_b(way, step)
        at = from_z(way, step - 1)
        src = tok.at[rows] if step == 1 else got.at[at, yl, rows]
        return rdma(src, got.at[at, yl, rows], s_zb.at[way, step - 1], r_zb.at[way, step - 1], z_dev[way])

    def zb_in(way, step):
        here = got.at[from_z(way, step), yl, rows_b(way, step)]
        return rdma(here, here, s_zb.at[way, step - 1], r_zb.at[way, step - 1], z_dev[way])

    def slot_of(way, step):
        return 2 * step - 1 + way if step else 0

    def yb(k, way, step):
        rows = rows_b(way, step)
        at = from_z(way, step)
        slot = slot_of(way, step)
        src = tok.at[rows] if step == 0 else got.at[at, yl, rows]
        return rdma(src, got.at[at, yl, rows], s_yb.at[k, slot], r_yb.at[k, slot], y_dev[k])

    def yb_in(k, way, step):
        slot = slot_of(way, step)
        here = got.at[from_z(way, step), lax.rem(yl + NYL - 1 - k, NYL), rows_b(way, step)]
        return rdma(here, here, s_yb.at[k, slot], r_yb.at[k, slot], y_dev[k])

    def each_yb(way, step, act):
        for k in range(3):
            act(yb(k, way, step))

    def start(copy):
        copy.start()

    def ya(k):
        rows = pl.ds(0, RA)
        at = lax.rem(lines[k] - yl + NYL, NYL) - 1
        return rdma(tok.at[rows], got.at[z, yl, rows], s_ya.at[at], r_ya.at[at], (d, lines[k] * NZ + z))

    def ya_in(k):
        at = lax.rem(yl - lines[k] + NYL, NYL) - 1
        here = got.at[z, lines[k], pl.ds(0, RA)]
        return rdma(here, here, s_ya.at[at], r_ya.at[at], z_dev[0])

    for way in (0, 1):
        za(way, 1, 0).start()
    for k in (1, 2, 3):
        ya(k).start()
    for way in (0, 1):
        zb(way, 1).start()
    each_yb(0, 0, start)

    load_tok.wait()
    shift[...] = jnp.broadcast_to(jnp.mean(got[z, yl].astype(F32), axis=1, keepdims=True), (SEQ, HD))

    def z_pass(step, k):
        for way in (0, 1):
            za_in(way, step, k).wait_recv()
            if step < FAR:
                za(way, step + 1, k).start()

    def b_pass(step):
        for way in (0, 1):
            zb_in(way, step).wait_recv()
            if step < FAR:
                zb(way, step + 1).start()
            each_yb(way, step, start)

    def y_in(step):
        for way in (0, 1) if step else (0,):
            for k in range(3):
                yb_in(k, way, step).wait_recv()

    def swap(zz):
        slot = zz // 6 * 3 + lax.rem(zz, 3)
        return rdma(got.at[zz], other.at[slot], s_n.at[slot], r_n.at[slot], core_dev)

    def process(zz, first):
        base = shift[...]
        one = jnp.zeros((SEQ, HD), F32) if first else total[...]
        two = jnp.zeros((SEQ, HD), F32) if first else square[...]
        for line in range(NYL):
            v = got[zz, line].astype(F32) - base
            one += v
            two += v * v
        total[...] = one
        square[...] = two

        @pl.when(lax.rem(zz // 3, 2) != core)
        def _():
            swap(zz).start()

    ready = []
    count = [0]

    def work():
        if ready:
            process(ready.pop(0), count[0] == 0)
            count[0] += 1

    for turn in range(1, FAR + 2):
        if turn <= FAR:
            b_pass(turn)
            z_pass(turn, 0)
        for k in (1, 2, 3):
            if turn == 1:
                ya_in(k).wait_recv()
                for way in (0, 1):
                    za(way, 1, k).start()
            else:
                z_pass(turn - 1, k)
            work()
        if turn == 1:
            for copy in small:
                copy.wait()
            for i, ref in enumerate((q_gain, k_gain)):
                column = jnp.broadcast_to(ref[...], (HD, HD)).T
                gains_t[i] = jnp.concatenate([column, column], axis=1)
            up_t[...] = d_attn[...].astype(F32).T.astype(BF16)
        if turn >= 2:
            step = turn - 2
            y_in(step)
            ready += [from_z(way, step) for way in ((0, 1) if step else (0,))]
    while len(ready) > 1:
        work()
    y_in(FAR)
    ready.append(from_z(0, FAR))
    while ready:
        work()

    moved = jnp.sum(total[...], axis=1, keepdims=True) / WIDTH
    spread = jnp.sum(square[...], axis=1, keepdims=True) / WIDTH - moved * moved
    mean = shift[:, 0:1] + moved
    rstd = lax.rsqrt(spread + 1e-06)
    mean_t = jnp.broadcast_to(mean, (SEQ, HD)).T
    rstd_t = jnp.broadcast_to(rstd, (SEQ, HD)).T
    mean_own[...] = mean_t[0:8]
    send_m = rdma(mean_own, mean_other, s_m.at[0], r_m.at[0], core_dev)
    send_m.start()
    total[...] = jnp.broadcast_to(mean, (SEQ, HD))
    square[...] = jnp.broadcast_to(rstd, (SEQ, HD))
    load_w.wait()
    projected = None
    for first in range(0, BLOCKS, 8):
        left = []
        for block in range(first, first + 8):
            v = got[block % NZ, block // NZ].astype(F32)
            v = (v - total[...]) * square[...] * gain[block : block + 1]
            left.append(v.astype(BF16))
        right = w[first : first + 8].reshape(8 * HD, COLS)
        term = nn(jnp.concatenate(left, axis=1), right)
        projected = term if projected is None else projected + term

    score_scale = 1.0 / math.sqrt(HD)
    gain_q = gains_t[0]
    gain_k = gains_t[1]
    q_t = projected[:, 0:HD].T
    k_t = projected[:, HD : 2 * HD].T
    values = projected[:, 2 * HD :].astype(BF16)
    q_hat, q_inv = head_norm(q_t)
    k_hat, k_inv = head_norm(k_t)
    q_n_t = (q_hat * gain_q).astype(BF16)
    k_n_f = k_hat * gain_k
    k_n_t = k_n_f.astype(BF16)
    k_n = k_n_f.T.astype(BF16)
    scores = nn(k_n, q_n_t) * score_scale
    grad_prob = nn(values, up_t[...])
    raised = jnp.exp(scores - jnp.max(scores, axis=0, keepdims=True))
    probs = raised * (1.0 / jnp.sum(raised, axis=0, keepdims=True))
    probs_low = probs.astype(BF16)
    grad_score = probs * (grad_prob - jnp.sum(probs * grad_prob, axis=0, keepdims=True))
    grad_score = (grad_score * score_scale).astype(BF16)
    grad_v = nt(up_t[...], probs_low)
    grad_kn = nt(q_n_t, grad_score)
    grad_qn = nn(k_n_t, grad_score)
    joined[0:HD] = (rstd_t * head_norm_back(grad_qn, q_hat, q_inv, gain_q)).astype(BF16)
    joined[HD : 2 * HD] = (rstd_t * head_norm_back(grad_kn, k_hat, k_inv, gain_k)).astype(BF16)
    joined[2 * HD :] = (rstd_t * grad_v).astype(BF16)
    send_j = rdma(joined, joined_other, s_j.at[0], r_j.at[0], core_dev)
    send_j.start()

    def swap_in(slot):
        return rdma(other.at[slot], other.at[slot], s_n.at[slot], r_n.at[slot], core_dev)

    for slot in range(SLOTS):
        swap_in(slot).wait_recv()
    send_m.wait_recv()
    send_j.wait_recv()
    off = joined[...].astype(F32) * mean_own[0:1] + joined_other[...].astype(F32) * mean_other[0:1]
    drift[...] = jnp.broadcast_to(jnp.sum(off, axis=1, keepdims=True), (COLS, HD))

    def grad_part(x_to, y_to, half):
        rows = pl.ds(half * HALF, HALF)
        left = jnp.concatenate([joined[rows], joined_other[rows]], axis=1)
        mine = jnp.concatenate([got[3 * (2 * y_to + core) + b, x_to] for b in range(3)], axis=1)
        theirs = jnp.concatenate([other[3 * y_to + b, x_to] for b in range(3)], axis=1)
        value = nn(left, jnp.concatenate([mine, theirs], axis=0))
        group = [gain[pl.ds(x_to * NZ + 3 * (2 * y_to + core) + b, 1)] for b in range(3)]
        away = drift[rows]
        return (value - jnp.concatenate([away] * 3, axis=1)) * jnp.concatenate(group, axis=1)

    x_next = [lax.rem(x + 1, NX), lax.rem(x + NX - 1, NX)]
    x_far = lax.rem(x + 2, NX)

    def x_copy(i, way, kind, q):
        at = (i, way, kind, q)
        return rdma(sx.at[at], rx.at[at], s_x.at[at], r_x.at[at], x_dev[way])

    def put(i, way, kind, value):
        value = value.astype(BF16)
        for q in (0, 1):
            sx[i, way, kind, q] = value[q * QUARTER : (q + 1) * QUARTER]

    def x_start(i, kind, q):
        for way in (0, 1):
            x_copy(i, way, kind, q).start()

    def relay(i, q):
        for way in (0, 1):
            x_copy(i, way, 0, q).wait_recv()
            sx[i, way, 2, q] = (part[i, way, q] + rx[i, way, 0, q].astype(F32)).astype(BF16)
            x_copy(i, way, 2, q).start()

    def later_parts(i, y_to):
        for way in (0, 1):
            value = grad_part(x_next[way], y_to, way)
            for q in (0, 1):
                part[i, way, q] = value[q * QUARTER : (q + 1) * QUARTER]
        for half in (0, 1):
            value = grad_part(x, y_to, half)
            for q in (0, 1):
                own[i, half, q] = value[q * QUARTER : (q + 1) * QUARTER]

    def gathered(i, half, q):
        x_copy(i, 1 - half, 1, q).wait_recv()
        x_copy(i, half, 2, q).wait_recv()
        return own[i, half, q] + rx[i, 1 - half, 1, q].astype(F32) + rx[i, half, 2, q].astype(F32)

    def y_copy(half, q):
        at = (half, q)
        return rdma(sy.at[at], ry.at[at], s_y.at[at], r_y.at[at], far_dev)

    def y_start(q):
        for half in (0, 1):
            sy[half, q] = gathered(0, half, q).astype(BF16)
            y_copy(half, q).start()

    for way in (0, 1):
        put(0, way, 0, grad_part(x_far, 1 - yh, way))
        x_copy(0, way, 0, 0).start()
    for way in (0, 1):
        put(0, way, 1, grad_part(x_next[way], 1 - yh, 1 - way))
        x_copy(0, way, 1, 0).start()
    x_start(0, 0, 1)
    later_parts(0, 1 - yh)
    for way in (0, 1):
        put(1, way, 0, grad_part(x_far, yh, way))
        put(1, way, 1, grad_part(x_next[way], yh, 1 - way))
    relay(0, 0)
    x_start(0, 1, 1)
    later_parts(1, yh)
    relay(0, 1)
    x_start(1, 0, 0)
    x_start(1, 1, 0)
    x_start(1, 0, 1)
    y_start(0)
    relay(1, 0)
    x_start(1, 1, 1)
    y_start(1)
    relay(1, 1)

    for way in (0, 1):
        for k in range(4):
            for step in range(1, FAR + 1):
                za(way, step, k).wait_send()
        for step in range(1, FAR + 1):
            zb(way, step).wait_send()
    for k in (1, 2, 3):
        ya(k).wait_send()
    for k in range(3):
        yb(k, 0, 0).wait_send()
        for step in range(1, FAR + 1):
            for way in (0, 1):
                yb(k, way, step).wait_send()
    for slot in range(SLOTS):
        swap_in(slot).wait_send()
    send_m.wait_send()
    send_j.wait_send()

    final = []
    for half in (0, 1):
        for q in (0, 1):
            value = gathered(1, half, q)
            y_copy(half, q).wait_recv()
            final.append(value + ry[half, q].astype(F32))
    final = jnp.concatenate(final, axis=0)
    for b in range(3):
        out[:, b * HD : (b + 1) * HD] = final[b * HD : (b + 1) * HD].T.astype(BF16)
    for i in (0, 1):
        for way in (0, 1):
            for kind in (0, 1, 2):
                for q in (0, 1):
                    x_copy(i, way, kind, q).wait_send()
    for half in (0, 1):
        for q in (0, 1):
            y_copy(half, q).wait_send()


def local(tokens, ln_gain, w_qkv, q_gain, k_gain, d_attn):
    dma = pltpu.SemaphoreType.DMA
    hbm = pl.BlockSpec(memory_space=pltpu.HBM)
    steps = 2 * FAR + 1
    pairs = []
    for shape in (
        (2, FAR, 4), (3,), (2, FAR), (3, steps), (SLOTS,), (1,), (1,), (2, 2, 3, 2), (2, 2),
    ):
        pairs += [dma(shape), dma(shape)]
    return pl.pallas_call(
        body,
        out_shape=jax.ShapeDtypeStruct((COLS, COLS), BF16),
        in_specs=[hbm] * 6,
        out_specs=pl.BlockSpec(memory_space=pltpu.VMEM),
        scratch_shapes=[
            pltpu.VMEM((NZ, NYL, SEQ, HD), BF16),
            pltpu.VMEM((SLOTS, NYL, SEQ, HD), BF16),
            pltpu.VMEM((BLOCKS, HD, COLS), BF16),
            pltpu.VMEM((BLOCKS, HD), F32),
            pltpu.VMEM((1, HD), F32),
            pltpu.VMEM((1, HD), F32),
            pltpu.VMEM((SEQ, HD), BF16),
            pltpu.VMEM((SEQ, HD), F32),
            pltpu.VMEM((SEQ, HD), F32),
            pltpu.VMEM((SEQ, HD), F32),
            pltpu.VMEM((COLS, SEQ), BF16),
            pltpu.VMEM((COLS, SEQ), BF16),
            pltpu.VMEM((8, SEQ), F32),
            pltpu.VMEM((8, SEQ), F32),
            pltpu.VMEM((COLS, HD), F32),
            pltpu.VMEM((HD, SEQ), BF16),
            pltpu.VMEM((2, HD, SEQ), F32),
            pltpu.VMEM((2, 2, 2, QUARTER, COLS), F32),
            pltpu.VMEM((2, 2, 2, QUARTER, COLS), F32),
            pltpu.VMEM((2, 2, 3, 2, QUARTER, COLS), BF16),
            pltpu.VMEM((2, 2, 3, 2, QUARTER, COLS), BF16),
            pltpu.VMEM((2, 2, QUARTER, COLS), BF16),
            pltpu.VMEM((2, 2, QUARTER, COLS), BF16),
            dma((6,)),
        ] + pairs,
        compiler_params=pltpu.CompilerParams(
            collective_id=0, has_side_effects=True, vmem_limit_bytes=48 * 2**20
        ),
        cost_estimate=pl.CostEstimate(flops=2_600_000_000, bytes_accessed=10_000_000, transcendentals=100_000),
        name="layer",
    )(
        *(
            pltpu.with_memory_space_constraint(array, pltpu.HBM)
            for array in (
                tokens, ln_gain.reshape(BLOCKS, HD), w_qkv.reshape(BLOCKS, HD, COLS), q_gain, k_gain, d_attn
            )
        )
    )


def solution(mesh):
    placed = (P("dp", "mp"), P(), P(None, "mp"), P("mp", None), P("mp", None), P("dp", "mp"))
    return jax.shard_map(
        local, mesh=mesh, in_specs=placed, out_specs=P("dp", "mp"), check_vma=False
    )
```

```python
import math

import jax
import jax.numpy as jnp
from jax import lax
from jax.experimental import pallas as pl
from jax.experimental.pallas import tpu as pltpu
from jax.sharding import PartitionSpec as P

MESH = pl.DeviceIdType.MESH
F32 = jnp.float32
BF16 = jnp.bfloat16
SEQ = 256
HD = 128
NX = 4
NYL = 4
NZ = 12
BLOCKS = NYL * NZ
WIDTH = BLOCKS * HD
COLS = 3 * HD
SLOTS = NZ // 2
FAR = NZ // 2
RA = 160
HA = 80
HB = 48
HALF = COLS // 2
CUTS = (4, 2)


ORDER = (
    ("a", 0, 1, 0), ("a", 1, 1, 0), ("b", 0, 1, 0), ("b", 1, 1, 0), ("l", 0, 0, 1), ("l", 0, 0, 2),
    ("a", 0, 2, 0), ("a", 1, 2, 0), ("b", 1, 2, 0), ("b", 0, 2, 0), ("l", 0, 0, 3), ("a", 0, 1, 1),
    ("a", 0, 1, 2), ("a", 1, 1, 1), ("a", 1, 1, 2), ("b", 1, 3, 0), ("b", 0, 3, 0), ("a", 0, 1, 3),
    ("a", 1, 1, 3), ("a", 0, 2, 1), ("a", 0, 3, 0), ("a", 1, 2, 1), ("a", 1, 2, 2), ("a", 1, 3, 0),
    ("a", 0, 2, 2), ("a", 0, 2, 3), ("a", 1, 2, 3), ("a", 0, 3, 1), ("y", 1, 1, 0), ("b", 0, 4, 0),
    ("b", 1, 4, 0), ("y", 1, 2, 0), ("a", 1, 3, 1), ("y", 0, 1, 0), ("a", 0, 3, 2), ("a", 1, 3, 2),
    ("a", 0, 3, 3), ("a", 1, 3, 3), ("a", 0, 4, 0), ("a", 1, 4, 0), ("b", 0, 5, 0), ("b", 1, 5, 0),
    ("a", 0, 4, 1), ("y", 0, 0, 0), ("a", 1, 4, 1), ("a", 0, 4, 2), ("a", 0, 4, 3), ("a", 1, 4, 2),
    ("y", 0, 4, 0), ("y", 0, 2, 0), ("a", 1, 4, 3), ("b", 1, 6, 0), ("a", 0, 5, 0), ("a", 1, 5, 0),
    ("b", 0, 6, 0), ("a", 0, 5, 1), ("a", 1, 5, 1), ("a", 1, 5, 2), ("a", 0, 5, 2), ("a", 0, 5, 3),
    ("a", 1, 5, 3), ("y", 1, 3, 0), ("a", 0, 6, 0), ("a", 1, 6, 1), ("y", 1, 5, 0), ("y", 0, 5, 0),
    ("y", 0, 3, 0), ("y", 1, 4, 0), ("a", 0, 6, 1), ("y", 1, 6, 0), ("a", 1, 6, 0), ("y", 0, 6, 0),
    ("a", 1, 6, 2), ("a", 0, 6, 2), ("a", 0, 6, 3), ("a", 1, 6, 3),
)


def rdma(src, dst, send, recv, device):
    return pltpu.make_async_remote_copy(
        src_ref=src, dst_ref=dst, send_sem=send, recv_sem=recv, device_id=device, device_id_type=MESH
    )


def head_norm(t):
    center = jnp.mean(t, axis=0, keepdims=True)
    moved = t - center
    spread = jnp.mean(moved * moved, axis=0, keepdims=True)
    inverse = lax.rsqrt(spread + 1e-06)
    return moved * inverse, inverse


def head_norm_back(grad, normal, inverse, gain):
    scaled = grad * gain
    first = jnp.mean(scaled, axis=0, keepdims=True)
    second = jnp.mean(scaled * normal, axis=0, keepdims=True)
    return inverse * (scaled - first - normal * second)


def nt(a, b):
    return lax.dot_general(a, b, (((1,), (1,)), ((), ())), preferred_element_type=F32)


def nn(a, b):
    return jnp.dot(a, b, preferred_element_type=F32)


def body(
    tok, gain_in, w_in, q_gain_in, k_gain_in, d_attn_in, out,
    got, other, w, gain, q_gain, k_gain, d_attn,
    shift, total, square, joined, joined_other, mean_own, mean_other, drift, up_t, gains_t,
    own, part, sx, rx, sy, ry, loads,
    s_za, r_za, s_ya, r_ya, s_zb, r_zb, s_yb, r_yb, s_n, r_n, s_m, r_m, s_j, r_j, s_x, r_x, s_y, r_y,
):
    d = lax.axis_index("dp")
    m = lax.axis_index("mp")
    core = lax.rem(d, 2)
    yh = lax.rem(d // 2, 2)
    x = d // 4
    yl = m // NZ
    z = lax.rem(m, NZ)

    z_dev = [(d, yl * NZ + lax.rem(z + hops, NZ)) for hops in (1, NZ - 1)]
    y_dev = [(d, lax.rem(yl + k, NYL) * NZ + z) for k in (1, 2, 3)]
    x_dev = [
        (lax.rem(x + 1, NX) * 4 + yh * 2 + core, m),
        (lax.rem(x + NX - 1, NX) * 4 + yh * 2 + core, m),
    ]
    core_dev = (d + 1 - 2 * core, m)
    far_dev = (x * 4 + (1 - yh) * 2 + core, m)

    def load(i, src, dst):
        return pltpu.make_async_copy(src, dst, loads.at[i])

    load_tok = load(0, tok, got.at[z, yl])
    load_w = load(1, w_in, w)
    small = [load(2, gain_in, gain), load(3, q_gain_in, q_gain), load(4, k_gain_in, k_gain), load(5, d_attn_in, d_attn)]
    load_tok.start()
    for copy in small:
        copy.start()
    load_w.start()

    barrier = pltpu.get_barrier_semaphore()
    partners = z_dev + y_dev + x_dev + [core_dev, far_dev]
    for device in partners:
        pl.semaphore_signal(barrier, inc=1, device_id=device, device_id_type=MESH)

    pl.semaphore_wait(barrier, len(partners))

    lines = [yl, yl + 1 - 2 * lax.rem(yl, 2), 2 - yl // 2, 3 - 3 * (yl // 2)]

    places = {(0, 0): z, (1, 0): z}
    for step in range(1, FAR + 1):
        places[0, step] = lax.rem(z + NZ - step, NZ)
        places[1, step] = lax.rem(z + step, NZ) if step < FAR else places[0, FAR]
    y_from = [lax.rem(yl + NYL - 1 - k, NYL) for k in range(3)]
    line_out = [0] + [lax.rem(lines[k] - yl + NYL, NYL) - 1 for k in (1, 2, 3)]
    line_in = [0] + [lax.rem(yl - lines[k] + NYL, NYL) - 1 for k in (1, 2, 3)]
    line_dev = [None] + [(d, lines[k] * NZ + z) for k in (1, 2, 3)]

    def from_z(way, step):
        return places[way, step]

    def rows_a(way, step):
        if step < FAR:
            return pl.ds(0, RA)
        return pl.ds(0, HA) if way == 0 else pl.ds(HA, RA - HA)

    def rows_b(way, step):
        if step < FAR:
            return pl.ds(RA, SEQ - RA)
        return pl.ds(RA, HB) if way == 0 else pl.ds(RA + HB, SEQ - RA - HB)

    def za(way, step, k):
        rows = rows_a(way, step)
        at = from_z(way, step - 1)
        src = tok.at[rows] if step == 1 and k == 0 else got.at[at, lines[k], rows]
        return rdma(src, got.at[at, lines[k], rows], s_za.at[way, step - 1, k], r_za.at[way, step - 1, k], z_dev[way])

    def za_in(way, step, k):
        here = got.at[from_z(way, step), lines[k], rows_a(way, step)]
        return rdma(here, here, s_za.at[way, step - 1, k], r_za.at[way, step - 1, k], z_dev[way])

    def zb(way, step):
        rows = rows_b(way, step)
        at = from_z(way, step - 1)
        src = tok.at[rows] if step == 1 else got.at[at, yl, rows]
        return rdma(src, got.at[at, yl, rows], s_zb.at[way, step - 1], r_zb.at[way, step - 1], z_dev[way])

    def zb_in(way, step):
        here = got.at[from_z(way, step), yl, rows_b(way, step)]
        return rdma(here, here, s_zb.at[way, step - 1], r_zb.at[way, step - 1], z_dev[way])

    def slot_of(way, step):
        return 2 * step - 1 + way if step else 0

    def yb(k, way, step):
        rows = rows_b(way, step)
        at = from_z(way, step)
        slot = slot_of(way, step)
        src = tok.at[rows] if step == 0 else got.at[at, yl, rows]
        return rdma(src, got.at[at, yl, rows], s_yb.at[k, slot], r_yb.at[k, slot], y_dev[k])

    def yb_in(k, way, step):
        slot = slot_of(way, step)
        here = got.at[from_z(way, step), y_from[k], rows_b(way, step)]
        return rdma(here, here, s_yb.at[k, slot], r_yb.at[k, slot], y_dev[k])

    def each_yb(way, step, act):
        for k in range(3):
            act(yb(k, way, step))

    def start(copy):
        copy.start()

    def ya(k):
        rows = pl.ds(0, RA)
        at = line_out[k]
        return rdma(tok.at[rows], got.at[z, yl, rows], s_ya.at[at], r_ya.at[at], line_dev[k])

    def ya_in(k):
        at = line_in[k]
        here = got.at[z, lines[k], pl.ds(0, RA)]
        return rdma(here, here, s_ya.at[at], r_ya.at[at], z_dev[0])

    for way in (0, 1):
        za(way, 1, 0).start()
    for k in (1, 2, 3):
        ya(k).start()
    for way in (0, 1):
        zb(way, 1).start()
    each_yb(0, 0, start)

    load_tok.wait()
    shift[...] = jnp.broadcast_to(jnp.mean(got[z, yl].astype(F32), axis=1, keepdims=True), (SEQ, HD))

    def z_pass(way, step, k):
        za_in(way, step, k).wait_recv()
        if step < FAR:
            za(way, step + 1, k).start()

    def b_pass(way, step):
        zb_in(way, step).wait_recv()
        if step < FAR:
            zb(way, step + 1).start()
        each_yb(way, step, start)

    def l_pass(k):
        ya_in(k).wait_recv()
        for way in (0, 1):
            za(way, 1, k).start()

    def y_in(way, step):
        for k in range(3):
            yb_in(k, way, step).wait_recv()

    def swap(zz):
        slot = zz // 6 * 3 + lax.rem(zz, 3)
        return rdma(got.at[zz], other.at[slot], s_n.at[slot], r_n.at[slot], core_dev)

    def process(zz, first):
        base = shift[...]
        one = jnp.zeros((SEQ, HD), F32) if first else total[...]
        two = jnp.zeros((SEQ, HD), F32) if first else square[...]
        for line in range(NYL):
            v = got[zz, line].astype(F32) - base
            one += v
            two += v * v
        total[...] = one
        square[...] = two

        @pl.when(lax.rem(zz // 3, 2) != core)
        def _():
            swap(zz).start()

    needs = {(0, 0): {("l", 0, 0, k) for k in (1, 2, 3)} | {("y", 0, 0, 0)}}
    for step in range(1, FAR + 1):
        for way in (0, 1):
            at = needs.setdefault((way if step < FAR else 0, step), set())
            at |= {("a", way, step, k) for k in range(4)} | {("b", way, step, 0), ("y", way, step, 0)}
    ready = []
    fresh = True
    for turn, item in enumerate(ORDER):
        kind, way, step, k = item
        if kind == "a":
            z_pass(way, step, k)
        elif kind == "b":
            b_pass(way, step)
        elif kind == "l":
            l_pass(k)
        else:
            y_in(way, step)
        for place, missing in needs.items():
            if item in missing:
                missing.remove(item)
                if not missing:
                    ready.append(place)
        if turn == 5:
            for copy in small:
                copy.wait()
            for i, ref in enumerate((q_gain, k_gain)):
                column = jnp.broadcast_to(ref[...], (HD, HD)).T
                gains_t[i] = jnp.concatenate([column, column], axis=1)
            up_t[...] = d_attn[...].astype(F32).T.astype(BF16)
        if ready:
            process(from_z(*ready.pop(0)), fresh)
            fresh = False
    for place in ready:
        process(from_z(*place), False)

    moved = jnp.sum(total[...], axis=1, keepdims=True) / WIDTH
    spread = jnp.sum(square[...], axis=1, keepdims=True) / WIDTH - moved * moved
    mean = shift[:, 0:1] + moved
    rstd = lax.rsqrt(spread + 1e-06)
    mean_t = jnp.broadcast_to(mean, (SEQ, HD)).T
    rstd_t = jnp.broadcast_to(rstd, (SEQ, HD)).T
    mean_own[...] = mean_t[0:8]
    send_m = rdma(mean_own, mean_other, s_m.at[0], r_m.at[0], core_dev)
    send_m.start()
    total[...] = jnp.broadcast_to(mean, (SEQ, HD))
    square[...] = jnp.broadcast_to(rstd, (SEQ, HD))
    load_w.wait()
    projected = None
    for first in range(0, BLOCKS, 8):
        left = []
        for block in range(first, first + 8):
            v = got[block % NZ, block // NZ].astype(F32)
            v = (v - total[...]) * square[...] * gain[block : block + 1]
            left.append(v.astype(BF16))
        right = w[first : first + 8].reshape(8 * HD, COLS)
        term = nn(jnp.concatenate(left, axis=1), right)
        projected = term if projected is None else projected + term

    score_scale = 1.0 / math.sqrt(HD)
    gain_q = gains_t[0]
    gain_k = gains_t[1]
    q_t = projected[:, 0:HD].T
    k_t = projected[:, HD : 2 * HD].T
    values = projected[:, 2 * HD :].astype(BF16)
    q_hat, q_inv = head_norm(q_t)
    k_hat, k_inv = head_norm(k_t)
    q_n_t = (q_hat * gain_q).astype(BF16)
    k_n_f = k_hat * gain_k
    k_n_t = k_n_f.astype(BF16)
    k_n = k_n_f.T.astype(BF16)
    scores = nn(k_n, q_n_t) * score_scale
    grad_prob = nn(values, up_t[...])
    raised = jnp.exp(scores - jnp.max(scores, axis=0, keepdims=True))
    probs = raised * (1.0 / jnp.sum(raised, axis=0, keepdims=True))
    probs_low = probs.astype(BF16)
    grad_score = probs * (grad_prob - jnp.sum(probs * grad_prob, axis=0, keepdims=True))
    grad_score = (grad_score * score_scale).astype(BF16)
    grad_v = nt(up_t[...], probs_low)
    grad_kn = nt(q_n_t, grad_score)
    grad_qn = nn(k_n_t, grad_score)
    joined[0:HD] = (rstd_t * head_norm_back(grad_qn, q_hat, q_inv, gain_q)).astype(BF16)
    joined[HD : 2 * HD] = (rstd_t * head_norm_back(grad_kn, k_hat, k_inv, gain_k)).astype(BF16)
    joined[2 * HD :] = (rstd_t * grad_v).astype(BF16)
    send_j = rdma(joined, joined_other, s_j.at[0], r_j.at[0], core_dev)
    send_j.start()

    def swap_in(slot):
        return rdma(other.at[slot], other.at[slot], s_n.at[slot], r_n.at[slot], core_dev)

    x_next = [lax.rem(x + 1, NX), lax.rem(x + NX - 1, NX)]
    x_far = lax.rem(x + 2, NX)

    def half_rows(half):
        return pl.ds(half * HALF, HALF)

    def mine(x_to, y_to):
        return jnp.concatenate([got[3 * (2 * y_to + core) + b, x_to] for b in range(3)], axis=1)

    def theirs(x_to, y_to):
        return jnp.concatenate([other[3 * y_to + b, x_to] for b in range(3)], axis=1)

    def corrected(value, x_to, y_to, half):
        group = [gain[pl.ds(x_to * NZ + 3 * (2 * y_to + core) + b, 1)] for b in range(3)]
        away = drift[half_rows(half)]
        return (value - jnp.concatenate([away] * 3, axis=1)) * jnp.concatenate(group, axis=1)

    def grad_part(x_to, y_to, half):
        rows = half_rows(half)
        left = jnp.concatenate([joined[rows], joined_other[rows]], axis=1)
        value = nn(left, jnp.concatenate([mine(x_to, y_to), theirs(x_to, y_to)], axis=0))
        return corrected(value, x_to, y_to, half)

    early = [nn(joined[half_rows(way)], mine(x_far, 1 - yh)) for way in (0, 1)]
    off = jnp.sum(joined[...].astype(F32) * mean_own[0:1], axis=1, keepdims=True)
    for slot in range(SLOTS):
        swap_in(slot).wait_recv()
    send_m.wait_recv()
    send_j.wait_recv()
    off += jnp.sum(joined_other[...].astype(F32) * mean_other[0:1], axis=1, keepdims=True)
    drift[...] = jnp.broadcast_to(off, (COLS, HD))

    def piece(i, q):
        size = HALF // CUTS[i]
        return pl.ds(q * size, size)

    def x_copy(i, way, kind, q):
        at = (i, way, kind, piece(i, q))
        sem = (i, way, kind, q)
        return rdma(sx.at[at], rx.at[at], s_x.at[sem], r_x.at[sem], x_dev[way])

    def x_start(i, kind, q):
        for way in (0, 1):
            x_copy(i, way, kind, q).start()

    def relay(i, q):
        rows = piece(i, q)
        for way in (0, 1):
            x_copy(i, way, 0, q).wait_recv()
            sx[i, way, 2, rows] = (part[i, way, rows] + rx[i, way, 0, rows].astype(F32)).astype(BF16)
            x_copy(i, way, 2, q).start()

    def later_parts(i, y_to):
        for way in (0, 1):
            part[i, way] = grad_part(x_next[way], y_to, way)
        for half in (0, 1):
            own[i, half] = grad_part(x, y_to, half)

    def gathered(i, half, q):
        rows = piece(i, q)
        x_copy(i, 1 - half, 1, q).wait_recv()
        x_copy(i, half, 2, q).wait_recv()
        return own[i, half, rows] + rx[i, 1 - half, 1, rows].astype(F32) + rx[i, half, 2, rows].astype(F32)

    def y_copy(half, q):
        at = (half, piece(0, q))
        return rdma(sy.at[at], ry.at[at], s_y.at[half, q], r_y.at[half, q], far_dev)

    def y_start(q):
        for half in (0, 1):
            sy[half, piece(0, q)] = gathered(0, half, q).astype(BF16)
            y_copy(half, q).start()

    for way in (0, 1):
        value = early[way] + nn(joined_other[half_rows(way)], theirs(x_far, 1 - yh))
        sx[0, way, 0] = corrected(value, x_far, 1 - yh, way).astype(BF16)
        x_copy(0, way, 0, 0).start()
    for way in (0, 1):
        sx[0, way, 1] = grad_part(x_next[way], 1 - yh, 1 - way).astype(BF16)
        x_copy(0, way, 1, 0).start()
    x_start(0, 0, 1)
    x_start(0, 1, 1)
    later_parts(0, 1 - yh)
    relay(0, 0)
    x_start(0, 0, 2)
    x_start(0, 1, 2)
    for way in (0, 1):
        sx[1, way, 0] = grad_part(x_far, yh, way).astype(BF16)
        sx[1, way, 1] = grad_part(x_next[way], yh, 1 - way).astype(BF16)
    relay(0, 1)
    x_start(0, 0, 3)
    x_start(0, 1, 3)
    y_start(0)
    relay(0, 2)
    x_start(1, 0, 0)
    later_parts(1, yh)
    y_start(1)
    relay(0, 3)
    x_start(1, 1, 0)
    x_start(1, 0, 1)
    y_start(2)
    relay(1, 0)
    x_start(1, 1, 1)
    y_start(3)
    relay(1, 1)

    for way in (0, 1):
        for k in range(4):
            for step in range(1, FAR + 1):
                za(way, step, k).wait_send()
        for step in range(1, FAR + 1):
            zb(way, step).wait_send()
    for k in (1, 2, 3):
        ya(k).wait_send()
    for k in range(3):
        yb(k, 0, 0).wait_send()
        for step in range(1, FAR + 1):
            for way in (0, 1):
                yb(k, way, step).wait_send()
    for slot in range(SLOTS):
        swap_in(slot).wait_send()
    send_m.wait_send()
    send_j.wait_send()

    final = []
    for half in (0, 1):
        for q in range(CUTS[1]):
            final.append(gathered(1, half, q))
    for half in (0, 1):
        for q in range(CUTS[0]):
            y_copy(half, q).wait_recv()
    final = jnp.concatenate(final, axis=0) + jnp.concatenate([ry[0], ry[1]], axis=0).astype(F32)
    for b in range(3):
        out[:, b * HD : (b + 1) * HD] = final[b * HD : (b + 1) * HD].T.astype(BF16)
    for i in (0, 1):
        for way in (0, 1):
            for kind in (0, 1, 2):
                for q in range(CUTS[i]):
                    x_copy(i, way, kind, q).wait_send()
    for half in (0, 1):
        for q in range(CUTS[0]):
            y_copy(half, q).wait_send()


def local(tokens, ln_gain, w_qkv, q_gain, k_gain, d_attn):
    dma = pltpu.SemaphoreType.DMA
    hbm = pl.BlockSpec(memory_space=pltpu.HBM)
    steps = 2 * FAR + 1
    pairs = []
    for shape in (
        (2, FAR, 4), (3,), (2, FAR), (3, steps), (SLOTS,), (1,), (1,), (2, 2, 3, CUTS[0]), (2, CUTS[0]),
    ):
        pairs += [dma(shape), dma(shape)]
    return pl.pallas_call(
        body,
        out_shape=jax.ShapeDtypeStruct((COLS, COLS), BF16),
        in_specs=[hbm] * 6,
        out_specs=pl.BlockSpec(memory_space=pltpu.VMEM),
        scratch_shapes=[
            pltpu.VMEM((NZ, NYL, SEQ, HD), BF16),
            pltpu.VMEM((SLOTS, NYL, SEQ, HD), BF16),
            pltpu.VMEM((BLOCKS, HD, COLS), BF16),
            pltpu.VMEM((BLOCKS, HD), F32),
            pltpu.VMEM((1, HD), F32),
            pltpu.VMEM((1, HD), F32),
            pltpu.VMEM((SEQ, HD), BF16),
            pltpu.VMEM((SEQ, HD), F32),
            pltpu.VMEM((SEQ, HD), F32),
            pltpu.VMEM((SEQ, HD), F32),
            pltpu.VMEM((COLS, SEQ), BF16),
            pltpu.VMEM((COLS, SEQ), BF16),
            pltpu.VMEM((8, SEQ), F32),
            pltpu.VMEM((8, SEQ), F32),
            pltpu.VMEM((COLS, HD), F32),
            pltpu.VMEM((HD, SEQ), BF16),
            pltpu.VMEM((2, HD, SEQ), F32),
            pltpu.VMEM((2, 2, HALF, COLS), F32),
            pltpu.VMEM((2, 2, HALF, COLS), F32),
            pltpu.VMEM((2, 2, 3, HALF, COLS), BF16),
            pltpu.VMEM((2, 2, 3, HALF, COLS), BF16),
            pltpu.VMEM((2, HALF, COLS), BF16),
            pltpu.VMEM((2, HALF, COLS), BF16),
            dma((6,)),
        ] + pairs,
        compiler_params=pltpu.CompilerParams(
            collective_id=0, has_side_effects=True, vmem_limit_bytes=48 * 2**20
        ),
        cost_estimate=pl.CostEstimate(flops=2_600_000_000, bytes_accessed=10_000_000, transcendentals=100_000),
        name="layer",
    )(
        *(
            pltpu.with_memory_space_constraint(array, pltpu.HBM)
            for array in (
                tokens, ln_gain.reshape(BLOCKS, HD), w_qkv.reshape(BLOCKS, HD, COLS), q_gain, k_gain, d_attn
            )
        )
    )


def solution(mesh):
    placed = (P("dp", "mp"), P(), P(None, "mp"), P("mp", None), P("mp", None), P("dp", "mp"))
    return jax.shard_map(
        local, mesh=mesh, in_specs=placed, out_specs=P("dp", "mp"), check_vma=False
    )
```

```python
import math

import jax
import jax.numpy as jnp
from jax import lax
from jax.experimental import pallas as pl
from jax.experimental.pallas import tpu as pltpu
from jax.sharding import PartitionSpec as P

MESH = pl.DeviceIdType.MESH
F32 = jnp.float32
BF16 = jnp.bfloat16
SEQ = 256
HD = 128
NX = 4
NYL = 4
NZ = 12
BLOCKS = NYL * NZ
WIDTH = BLOCKS * HD
COLS = 3 * HD
SLOTS = NZ // 2
FAR = NZ // 2
RA = 160
HA = 80
HB = 48
HALF = COLS // 2
CUTS = (4, 2)


ORDER = (
    ("b", 0, 1, 0), ("b", 1, 1, 0), ("a", 0, 1, 0), ("a", 1, 1, 0), ("l", 0, 0, 1), ("l", 0, 0, 2),
    ("l", 0, 0, 3), ("b", 0, 2, 0), ("b", 1, 2, 0), ("a", 0, 2, 0), ("a", 1, 2, 0), ("a", 0, 1, 1),
    ("a", 1, 1, 1), ("a", 0, 1, 2), ("a", 1, 1, 2), ("a", 0, 1, 3), ("a", 1, 1, 3), ("y", 0, 0, 0),
    ("b", 0, 3, 0), ("b", 1, 3, 0), ("a", 0, 3, 0), ("a", 1, 3, 0), ("a", 0, 2, 1), ("a", 1, 2, 1),
    ("a", 0, 2, 2), ("a", 1, 2, 2), ("a", 0, 2, 3), ("a", 1, 2, 3), ("y", 0, 1, 0), ("y", 1, 1, 0),
    ("b", 0, 4, 0), ("b", 1, 4, 0), ("a", 0, 4, 0), ("a", 1, 4, 0), ("a", 0, 3, 1), ("a", 1, 3, 1),
    ("a", 0, 3, 2), ("a", 1, 3, 2), ("a", 0, 3, 3), ("a", 1, 3, 3), ("y", 0, 2, 0), ("y", 1, 2, 0),
    ("b", 0, 5, 0), ("b", 1, 5, 0), ("a", 0, 5, 0), ("a", 1, 5, 0), ("a", 0, 4, 1), ("a", 1, 4, 1),
    ("a", 0, 4, 2), ("a", 1, 4, 2), ("a", 0, 4, 3), ("a", 1, 4, 3), ("y", 0, 3, 0), ("y", 1, 3, 0),
    ("b", 0, 6, 0), ("b", 1, 6, 0), ("a", 0, 6, 0), ("a", 1, 6, 0), ("a", 0, 5, 1), ("a", 1, 5, 1),
    ("a", 0, 5, 2), ("a", 1, 5, 2), ("a", 0, 5, 3), ("a", 1, 5, 3), ("y", 0, 4, 0), ("y", 1, 4, 0),
    ("a", 0, 6, 1), ("a", 1, 6, 1), ("a", 0, 6, 2), ("a", 1, 6, 2), ("a", 0, 6, 3), ("a", 1, 6, 3),
    ("y", 0, 5, 0), ("y", 1, 5, 0), ("y", 0, 6, 0), ("y", 1, 6, 0),
)


def rdma(src, dst, send, recv, device):
    return pltpu.make_async_remote_copy(
        src_ref=src, dst_ref=dst, send_sem=send, recv_sem=recv, device_id=device, device_id_type=MESH
    )


def head_norm(t):
    center = jnp.mean(t, axis=0, keepdims=True)
    moved = t - center
    spread = jnp.mean(moved * moved, axis=0, keepdims=True)
    inverse = lax.rsqrt(spread + 1e-06)
    return moved * inverse, inverse


def head_norm_back(grad, normal, inverse, gain):
    scaled = grad * gain
    first = jnp.mean(scaled, axis=0, keepdims=True)
    second = jnp.mean(scaled * normal, axis=0, keepdims=True)
    return inverse * (scaled - first - normal * second)


def nt(a, b):
    return lax.dot_general(a, b, (((1,), (1,)), ((), ())), preferred_element_type=F32)


def nn(a, b):
    return jnp.dot(a, b, preferred_element_type=F32)


def body(
    tok, gain_in, w_in, q_gain_in, k_gain_in, d_attn_in, out,
    got, other, w, gain, q_gain, k_gain, d_attn,
    shift, total, square, joined, joined_other, mean_own, mean_other, drift, up_t, gains_t,
    own, part, sx, rx, sy, ry, loads,
    s_za, r_za, s_ya, r_ya, s_zb, r_zb, s_yb, r_yb, s_n, r_n, s_m, r_m, s_j, r_j, s_x, r_x, s_y, r_y,
):
    d = lax.axis_index("dp")
    m = lax.axis_index("mp")
    core = lax.rem(d, 2)
    yh = lax.rem(d // 2, 2)
    x = d // 4
    yl = m // NZ
    z = lax.rem(m, NZ)

    z_dev = [(d, yl * NZ + lax.rem(z + hops, NZ)) for hops in (1, NZ - 1)]
    y_dev = [(d, lax.rem(yl + k, NYL) * NZ + z) for k in (1, 2, 3)]
    x_dev = [
        (lax.rem(x + 1, NX) * 4 + yh * 2 + core, m),
        (lax.rem(x + NX - 1, NX) * 4 + yh * 2 + core, m),
    ]
    core_dev = (d + 1 - 2 * core, m)
    far_dev = (x * 4 + (1 - yh) * 2 + core, m)

    def load(i, src, dst):
        return pltpu.make_async_copy(src, dst, loads.at[i])

    load_tok = load(0, tok, got.at[z, yl])
    load_w = load(1, w_in, w)
    small = [load(2, gain_in, gain), load(3, q_gain_in, q_gain), load(4, k_gain_in, k_gain), load(5, d_attn_in, d_attn)]
    load_tok.start()
    for copy in small:
        copy.start()
    load_w.start()

    barrier = pltpu.get_barrier_semaphore()
    partners = z_dev + y_dev + x_dev + [core_dev, far_dev]
    for device in partners:
        pl.semaphore_signal(barrier, inc=1, device_id=device, device_id_type=MESH)

    pl.semaphore_wait(barrier, len(partners))

    lines = [yl, yl + 1 - 2 * lax.rem(yl, 2), 2 - yl // 2, 3 - 3 * (yl // 2)]

    places = {(0, 0): z, (1, 0): z}
    for step in range(1, FAR + 1):
        places[0, step] = lax.rem(z + NZ - step, NZ)
        places[1, step] = lax.rem(z + step, NZ) if step < FAR else places[0, FAR]
    y_from = [lax.rem(yl + NYL - 1 - k, NYL) for k in range(3)]
    line_out = [0] + [lax.rem(lines[k] - yl + NYL, NYL) - 1 for k in (1, 2, 3)]
    line_in = [0] + [lax.rem(yl - lines[k] + NYL, NYL) - 1 for k in (1, 2, 3)]
    line_dev = [None] + [(d, lines[k] * NZ + z) for k in (1, 2, 3)]

    def from_z(way, step):
        return places[way, step]

    def rows_a(way, step):
        if step < FAR:
            return pl.ds(0, RA)
        return pl.ds(0, HA) if way == 0 else pl.ds(HA, RA - HA)

    def rows_b(way, step):
        if step < FAR:
            return pl.ds(RA, SEQ - RA)
        return pl.ds(RA, HB) if way == 0 else pl.ds(RA + HB, SEQ - RA - HB)

    def za(way, step, k):
        rows = rows_a(way, step)
        at = from_z(way, step - 1)
        src = tok.at[rows] if step == 1 and k == 0 else got.at[at, lines[k], rows]
        return rdma(src, got.at[at, lines[k], rows], s_za.at[way, step - 1, k], r_za.at[way, step - 1, k], z_dev[way])

    def za_in(way, step, k):
        here = got.at[from_z(way, step), lines[k], rows_a(way, step)]
        return rdma(here, here, s_za.at[way, step - 1, k], r_za.at[way, step - 1, k], z_dev[way])

    def zb(way, step):
        rows = rows_b(way, step)
        at = from_z(way, step - 1)
        src = tok.at[rows] if step == 1 else got.at[at, yl, rows]
        return rdma(src, got.at[at, yl, rows], s_zb.at[way, step - 1], r_zb.at[way, step - 1], z_dev[way])

    def zb_in(way, step):
        here = got.at[from_z(way, step), yl, rows_b(way, step)]
        return rdma(here, here, s_zb.at[way, step - 1], r_zb.at[way, step - 1], z_dev[way])

    def slot_of(way, step):
        return 2 * step - 1 + way if step else 0

    def yb(k, way, step):
        rows = rows_b(way, step)
        at = from_z(way, step)
        slot = slot_of(way, step)
        src = tok.at[rows] if step == 0 else got.at[at, yl, rows]
        return rdma(src, got.at[at, yl, rows], s_yb.at[k, slot], r_yb.at[k, slot], y_dev[k])

    def yb_in(k, way, step):
        slot = slot_of(way, step)
        here = got.at[from_z(way, step), y_from[k], rows_b(way, step)]
        return rdma(here, here, s_yb.at[k, slot], r_yb.at[k, slot], y_dev[k])

    def each_yb(way, step, act):
        for k in range(3):
            act(yb(k, way, step))

    def start(copy):
        copy.start()

    def ya(k):
        rows = pl.ds(0, RA)
        at = line_out[k]
        return rdma(tok.at[rows], got.at[z, yl, rows], s_ya.at[at], r_ya.at[at], line_dev[k])

    def ya_in(k):
        at = line_in[k]
        here = got.at[z, lines[k], pl.ds(0, RA)]
        return rdma(here, here, s_ya.at[at], r_ya.at[at], z_dev[0])

    for way in (0, 1):
        za(way, 1, 0).start()
    for k in (1, 2, 3):
        ya(k).start()
    for way in (0, 1):
        zb(way, 1).start()
    each_yb(0, 0, start)

    load_tok.wait()
    shift[...] = jnp.broadcast_to(jnp.mean(got[z, yl].astype(F32), axis=1, keepdims=True), (SEQ, HD))

    def z_pass(way, step, k):
        za_in(way, step, k).wait_recv()
        if step < FAR:
            za(way, step + 1, k).start()

    def b_pass(way, step):
        zb_in(way, step).wait_recv()
        if step < FAR:
            zb(way, step + 1).start()
        each_yb(way, step, start)

    def l_pass(k):
        ya_in(k).wait_recv()
        for way in (0, 1):
            za(way, 1, k).start()

    def y_in(way, step):
        for k in range(3):
            yb_in(k, way, step).wait_recv()

    def swap(zz):
        slot = zz // 6 * 3 + lax.rem(zz, 3)
        return rdma(got.at[zz], other.at[slot], s_n.at[slot], r_n.at[slot], core_dev)

    def process(zz, first):
        base = shift[...]
        one = jnp.zeros((SEQ, HD), F32) if first else total[...]
        two = jnp.zeros((SEQ, HD), F32) if first else square[...]
        for line in range(NYL):
            v = got[zz, line].astype(F32) - base
            one += v
            two += v * v
        total[...] = one
        square[...] = two

        @pl.when(lax.rem(zz // 3, 2) != core)
        def _():
            swap(zz).start()

    needs = {(0, 0): {("l", 0, 0, k) for k in (1, 2, 3)} | {("y", 0, 0, 0)}}
    for step in range(1, FAR + 1):
        for way in (0, 1):
            at = needs.setdefault((way if step < FAR else 0, step), set())
            at |= {("a", way, step, k) for k in range(4)} | {("b", way, step, 0), ("y", way, step, 0)}
    ready = []
    fresh = True
    for turn, item in enumerate(ORDER):
        kind, way, step, k = item
        if kind == "a":
            z_pass(way, step, k)
        elif kind == "b":
            b_pass(way, step)
        elif kind == "l":
            l_pass(k)
        else:
            y_in(way, step)
        for place, missing in needs.items():
            if item in missing:
                missing.remove(item)
                if not missing:
                    ready.append(place)
        if turn == 5:
            for copy in small:
                copy.wait()
            for i, ref in enumerate((q_gain, k_gain)):
                column = jnp.broadcast_to(ref[...], (HD, HD)).T
                gains_t[i] = jnp.concatenate([column, column], axis=1)
            up_t[...] = d_attn[...].astype(F32).T.astype(BF16)
        if ready:
            process(from_z(*ready.pop(0)), fresh)
            fresh = False
    for place in ready:
        process(from_z(*place), False)

    moved = jnp.sum(total[...], axis=1, keepdims=True) / WIDTH
    spread = jnp.sum(square[...], axis=1, keepdims=True) / WIDTH - moved * moved
    mean = shift[:, 0:1] + moved
    rstd = lax.rsqrt(spread + 1e-06)
    mean_t = jnp.broadcast_to(mean, (SEQ, HD)).T
    rstd_t = jnp.broadcast_to(rstd, (SEQ, HD)).T
    mean_own[...] = mean_t[0:8]
    send_m = rdma(mean_own, mean_other, s_m.at[0], r_m.at[0], core_dev)
    send_m.start()
    total[...] = jnp.broadcast_to(mean, (SEQ, HD))
    square[...] = jnp.broadcast_to(rstd, (SEQ, HD))
    load_w.wait()
    projected = None
    for first in range(0, BLOCKS, 8):
        left = []
        for block in range(first, first + 8):
            v = got[block % NZ, block // NZ].astype(F32)
            v = (v - total[...]) * square[...] * gain[block : block + 1]
            left.append(v.astype(BF16))
        right = w[first : first + 8].reshape(8 * HD, COLS)
        term = nn(jnp.concatenate(left, axis=1), right)
        projected = term if projected is None else projected + term

    score_scale = 1.0 / math.sqrt(HD)
    gain_q = gains_t[0]
    gain_k = gains_t[1]
    q_t = projected[:, 0:HD].T
    k_t = projected[:, HD : 2 * HD].T
    values = projected[:, 2 * HD :].astype(BF16)
    q_hat, q_inv = head_norm(q_t)
    k_hat, k_inv = head_norm(k_t)
    q_n_t = (q_hat * gain_q).astype(BF16)
    k_n_f = k_hat * gain_k
    k_n_t = k_n_f.astype(BF16)
    k_n = k_n_f.T.astype(BF16)
    scores = nn(k_n, q_n_t) * score_scale
    grad_prob = nn(values, up_t[...])
    raised = jnp.exp(scores - jnp.max(scores, axis=0, keepdims=True))
    probs = raised * (1.0 / jnp.sum(raised, axis=0, keepdims=True))
    probs_low = probs.astype(BF16)
    grad_score = probs * (grad_prob - jnp.sum(probs * grad_prob, axis=0, keepdims=True))
    grad_score = (grad_score * score_scale).astype(BF16)
    grad_v = nt(up_t[...], probs_low)
    grad_kn = nt(q_n_t, grad_score)
    grad_qn = nn(k_n_t, grad_score)
    joined[0:HD] = (rstd_t * head_norm_back(grad_qn, q_hat, q_inv, gain_q)).astype(BF16)
    joined[HD : 2 * HD] = (rstd_t * head_norm_back(grad_kn, k_hat, k_inv, gain_k)).astype(BF16)
    joined[2 * HD :] = (rstd_t * grad_v).astype(BF16)
    send_j = rdma(joined, joined_other, s_j.at[0], r_j.at[0], core_dev)
    send_j.start()

    def swap_in(slot):
        return rdma(other.at[slot], other.at[slot], s_n.at[slot], r_n.at[slot], core_dev)

    x_next = [lax.rem(x + 1, NX), lax.rem(x + NX - 1, NX)]
    x_far = lax.rem(x + 2, NX)

    def half_rows(half):
        return pl.ds(half * HALF, HALF)

    def mine(x_to, y_to):
        return jnp.concatenate([got[3 * (2 * y_to + core) + b, x_to] for b in range(3)], axis=1)

    def theirs(x_to, y_to):
        return jnp.concatenate([other[3 * y_to + b, x_to] for b in range(3)], axis=1)

    def corrected(value, x_to, y_to, half):
        group = [gain[pl.ds(x_to * NZ + 3 * (2 * y_to + core) + b, 1)] for b in range(3)]
        away = drift[half_rows(half)]
        return (value - jnp.concatenate([away] * 3, axis=1)) * jnp.concatenate(group, axis=1)

    def grad_part(x_to, y_to, half):
        rows = half_rows(half)
        left = jnp.concatenate([joined[rows], joined_other[rows]], axis=1)
        value = nn(left, jnp.concatenate([mine(x_to, y_to), theirs(x_to, y_to)], axis=0))
        return corrected(value, x_to, y_to, half)

    early = [nn(joined[half_rows(way)], mine(x_far, 1 - yh)) for way in (0, 1)]
    off = jnp.sum(joined[...].astype(F32) * mean_own[0:1], axis=1, keepdims=True)
    for slot in range(SLOTS):
        swap_in(slot).wait_recv()
    send_m.wait_recv()
    send_j.wait_recv()
    off += jnp.sum(joined_other[...].astype(F32) * mean_other[0:1], axis=1, keepdims=True)
    drift[...] = jnp.broadcast_to(off, (COLS, HD))

    def piece(i, q):
        size = HALF // CUTS[i]
        return pl.ds(q * size, size)

    def x_copy(i, way, kind, q):
        at = (i, way, kind, piece(i, q))
        sem = (i, way, kind, q)
        return rdma(sx.at[at], rx.at[at], s_x.at[sem], r_x.at[sem], x_dev[way])

    def x_start(i, kind, q):
        for way in (0, 1):
            x_copy(i, way, kind, q).start()

    def relay(i, q):
        rows = piece(i, q)
        for way in (0, 1):
            x_copy(i, way, 0, q).wait_recv()
            sx[i, way, 2, rows] = (part[i, way, rows] + rx[i, way, 0, rows].astype(F32)).astype(BF16)
            x_copy(i, way, 2, q).start()

    def later_parts(i, y_to):
        for way in (0, 1):
            part[i, way] = grad_part(x_next[way], y_to, way)
        for half in (0, 1):
            own[i, half] = grad_part(x, y_to, half)

    def gathered(i, half, q):
        rows = piece(i, q)
        x_copy(i, 1 - half, 1, q).wait_recv()
        x_copy(i, half, 2, q).wait_recv()
        return own[i, half, rows] + rx[i, 1 - half, 1, rows].astype(F32) + rx[i, half, 2, rows].astype(F32)

    def y_copy(half, q):
        at = (half, piece(0, q))
        return rdma(sy.at[at], ry.at[at], s_y.at[half, q], r_y.at[half, q], far_dev)

    def y_start(q):
        for half in (0, 1):
            sy[half, piece(0, q)] = gathered(0, half, q).astype(BF16)
            y_copy(half, q).start()

    for way in (0, 1):
        value = early[way] + nn(joined_other[half_rows(way)], theirs(x_far, 1 - yh))
        sx[0, way, 0] = corrected(value, x_far, 1 - yh, way).astype(BF16)
        x_copy(0, way, 0, 0).start()
    for way in (0, 1):
        sx[0, way, 1] = grad_part(x_next[way], 1 - yh, 1 - way).astype(BF16)
        x_copy(0, way, 1, 0).start()
    x_start(0, 0, 1)
    x_start(0, 1, 1)
    later_parts(0, 1 - yh)
    relay(0, 0)
    x_start(0, 0, 2)
    x_start(0, 1, 2)
    for way in (0, 1):
        sx[1, way, 0] = grad_part(x_far, yh, way).astype(BF16)
        sx[1, way, 1] = grad_part(x_next[way], yh, 1 - way).astype(BF16)
    relay(0, 1)
    x_start(0, 0, 3)
    x_start(0, 1, 3)
    y_start(0)
    relay(0, 2)
    x_start(1, 0, 0)
    later_parts(1, yh)
    y_start(1)
    relay(0, 3)
    x_start(1, 1, 0)
    x_start(1, 0, 1)
    y_start(2)
    relay(1, 0)
    x_start(1, 1, 1)
    y_start(3)
    relay(1, 1)

    for way in (0, 1):
        for k in range(4):
            for step in range(1, FAR + 1):
                za(way, step, k).wait_send()
        for step in range(1, FAR + 1):
            zb(way, step).wait_send()
    for k in (1, 2, 3):
        ya(k).wait_send()
    for k in range(3):
        yb(k, 0, 0).wait_send()
        for step in range(1, FAR + 1):
            for way in (0, 1):
                yb(k, way, step).wait_send()
    for slot in range(SLOTS):
        swap_in(slot).wait_send()
    send_m.wait_send()
    send_j.wait_send()

    final = []
    for half in (0, 1):
        for q in range(CUTS[1]):
            final.append(gathered(1, half, q))
    for half in (0, 1):
        for q in range(CUTS[0]):
            y_copy(half, q).wait_recv()
    final = jnp.concatenate(final, axis=0) + jnp.concatenate([ry[0], ry[1]], axis=0).astype(F32)
    for b in range(3):
        out[:, b * HD : (b + 1) * HD] = final[b * HD : (b + 1) * HD].T.astype(BF16)
    for i in (0, 1):
        for way in (0, 1):
            for kind in (0, 1, 2):
                for q in range(CUTS[i]):
                    x_copy(i, way, kind, q).wait_send()
    for half in (0, 1):
        for q in range(CUTS[0]):
            y_copy(half, q).wait_send()


def local(tokens, ln_gain, w_qkv, q_gain, k_gain, d_attn):
    dma = pltpu.SemaphoreType.DMA
    hbm = pl.BlockSpec(memory_space=pltpu.HBM)
    steps = 2 * FAR + 1
    pairs = []
    for shape in (
        (2, FAR, 4), (3,), (2, FAR), (3, steps), (SLOTS,), (1,), (1,), (2, 2, 3, CUTS[0]), (2, CUTS[0]),
    ):
        pairs += [dma(shape), dma(shape)]
    return pl.pallas_call(
        body,
        out_shape=jax.ShapeDtypeStruct((COLS, COLS), BF16),
        in_specs=[hbm] * 6,
        out_specs=pl.BlockSpec(memory_space=pltpu.VMEM),
        scratch_shapes=[
            pltpu.VMEM((NZ, NYL, SEQ, HD), BF16),
            pltpu.VMEM((SLOTS, NYL, SEQ, HD), BF16),
            pltpu.VMEM((BLOCKS, HD, COLS), BF16),
            pltpu.VMEM((BLOCKS, HD), F32),
            pltpu.VMEM((1, HD), F32),
            pltpu.VMEM((1, HD), F32),
            pltpu.VMEM((SEQ, HD), BF16),
            pltpu.VMEM((SEQ, HD), F32),
            pltpu.VMEM((SEQ, HD), F32),
            pltpu.VMEM((SEQ, HD), F32),
            pltpu.VMEM((COLS, SEQ), BF16),
            pltpu.VMEM((COLS, SEQ), BF16),
            pltpu.VMEM((8, SEQ), F32),
            pltpu.VMEM((8, SEQ), F32),
            pltpu.VMEM((COLS, HD), F32),
            pltpu.VMEM((HD, SEQ), BF16),
            pltpu.VMEM((2, HD, SEQ), F32),
            pltpu.VMEM((2, 2, HALF, COLS), F32),
            pltpu.VMEM((2, 2, HALF, COLS), F32),
            pltpu.VMEM((2, 2, 3, HALF, COLS), BF16),
            pltpu.VMEM((2, 2, 3, HALF, COLS), BF16),
            pltpu.VMEM((2, HALF, COLS), BF16),
            pltpu.VMEM((2, HALF, COLS), BF16),
            dma((6,)),
        ] + pairs,
        compiler_params=pltpu.CompilerParams(
            collective_id=0, has_side_effects=True, vmem_limit_bytes=48 * 2**20
        ),
        cost_estimate=pl.CostEstimate(flops=2_600_000_000, bytes_accessed=10_000_000, transcendentals=100_000),
        name="layer",
    )(
        *(
            pltpu.with_memory_space_constraint(array, pltpu.HBM)
            for array in (
                tokens, ln_gain.reshape(BLOCKS, HD), w_qkv.reshape(BLOCKS, HD, COLS), q_gain, k_gain, d_attn
            )
        )
    )


def solution(mesh):
    placed = (P("dp", "mp"), P(), P(None, "mp"), P("mp", None), P("mp", None), P("dp", "mp"))
    return jax.shard_map(
        local, mesh=mesh, in_specs=placed, out_specs=P("dp", "mp"), check_vma=False
    )
```
